32 devices in a mesh: grp: 2 (over y), path: 4 (over z), scen: 2 (over x), sub: 2 (over core).
Axes of the slice: x: 2, y: 2, z: 4, core: 2. Of those that a mesh axis runs over, the one named last changes fastest.
Arguments:
- path_links: int32 [8, 16384], P(None, ('grp', 'path')), parts along dimension 1, may hold values from -1 to 3583, as said below
- block_tiles: int32 [128, 16], P(('grp', 'path')), parts along dimension 0, may hold values from 0 to 27, as said below
- block_count: int32 [128], P(('grp', 'path')), parts along dimension 0, may hold values from 1 to 16
- path_commodity: int32 [128, 128], P(('grp', 'path')), parts along dimension 0, may hold values from 0 to 31, never falling along the last dimension, each value on 1 to 8 neighbouring positions
- demand: int32 [256, 4096], P(('scen', 'sub'), ('grp', 'path')), parts along dimension 1, may hold values from 1 to 64
- lengths: float32 [256, 7168], P(('scen', 'sub'), ('grp', 'path')), parts along dimension 1, may hold values from 0.05 to 10
- capacity: float32 [7168], P(('grp', 'path')), parts along dimension 0, may hold values from 4 to 32
- scenario_weight: float32 [512], P(('grp', 'scen', 'sub')), parts along dimension 0, may hold values from 0.5 to 2
Outputs:
- flows: float32 [256, 16384], P(('scen', 'sub'), ('grp', 'path')), parts along dimension 1
- lengths_next: float32 [256, 7168], P(('scen', 'sub'), ('grp', 'path')), parts along dimension 1
- robust_cost: float32 [16384], P(('grp', 'path')), parts along dimension 0
The draws below stay inside these ranges and needn't reach their ends.
There are 2 independent parts, one for each index of `grp`. The reference program is written for one: setup_inputs(seed, part) draws one part's arguments, and reference() takes and returns one part's arrays. A program takes and returns all parts, laid end to end along the dimension named above; each array names one. Nothing has to cross between parts.
Inputs may be any that keep to these rules, and one draw needn't show every extreme that they name: `path_links`: entry [h, p] is the link of hop h of path p, or -1 past the path's last hop (hop 0 is never -1). Every link of a path in block b = p // 128 lies in a link block named by block_tiles[b, 0] to block_tiles[b, block_count[b] - 1]; link block j holds links j * 128 to (j + 1) * 128 - 1. `block_tiles`: the entries of one row are distinct link blocks.
All inputs are finite; a program needn't handle non-finite values.
Results may differ from the reference program's by a relative error of at most 0.0003.
Values sent between devices are 32-bit elements; how exact they have to be, the bound alone decides.
No kernel may reach another device: no remote copies, remote signals or barrier semaphores. Data moves between devices by JAX's collectives and lax.ppermute only.
A program may use at most 64 MiB of HBM per device.

```python
import math
import jax
import jax.numpy as jnp
import numpy as np
from jax import lax

PATHS_PER_BLOCK = 128
LB = 128
HOPS = 8
MAXT = 16
COMMODITY_BLOCK = 32
S = 256
BLOCK_TOTAL = 64
COMM = 2048
NLB = 28
L = 3584


def network(key):
    keys = jax.random.split(jax.random.fold_in(key, 11), 6)
    shuffled = jax.vmap(lambda sub_key: jax.random.permutation(sub_key, NLB))(jax.random.split(keys[0], BLOCK_TOTAL))[:, :MAXT]
    full_block = jax.random.randint(keys[1], (), 0, BLOCK_TOTAL)
    offset = NLB - 1 - shuffled[full_block, 0]
    tile_ids = ((shuffled + offset) % NLB).astype(jnp.int32)
    shrink = jax.random.randint(keys[2], (BLOCK_TOTAL,), 0, 4)
    counts = jnp.maximum(jnp.right_shift(jnp.full((BLOCK_TOTAL,), MAXT, jnp.int32), shrink), 1)
    counts = counts.at[full_block].set(MAXT)
    slot_pick = jax.random.randint(keys[3], (HOPS, BLOCK_TOTAL, PATHS_PER_BLOCK), 0, MAXT) % counts[None, :, None]
    picked = jnp.take_along_axis(jnp.broadcast_to(tile_ids[None], (HOPS, BLOCK_TOTAL, MAXT)), slot_pick, axis=2)
    hop_links = picked * LB + jax.random.randint(keys[4], (HOPS, BLOCK_TOTAL, PATHS_PER_BLOCK), 0, LB)
    hop_links = hop_links.at[0, full_block, 0].set(NLB * LB - 1)
    path_length = jax.random.randint(keys[5], (BLOCK_TOTAL, PATHS_PER_BLOCK), 1, HOPS + 1)
    path_length = path_length.at[full_block, 1].set(1)
    hop_index = jnp.arange(HOPS)[:, None, None]
    hop_links = jnp.where(hop_index < path_length[None], hop_links, -1)
    return (tile_ids, counts.astype(jnp.int32), hop_links.reshape(HOPS, BLOCK_TOTAL * PATHS_PER_BLOCK).astype(jnp.int32))


def draw_path_links(key, part):
    return network(key)[2]


def draw_block_tiles(key, part):
    return network(key)[0]


def draw_block_count(key, part):
    return network(key)[1]


def draw_lengths(key, part):
    base_draw = jax.random.uniform(jax.random.fold_in(key, 21), (S, L), jnp.float32, -1.0, 1.0)
    position = jnp.arange(L, dtype=jnp.float32) / (L - 1)
    return 0.5 * jnp.exp(0.8 * base_draw) * (1.0 + 2.0 * position)[None, :]


def touch_ends(entries, own_key, low, top_value):
    spot = [jax.random.randint(jax.random.fold_in(own_key, axis), (), 0, length) for axis, length in enumerate(entries.shape)]
    main_axis = entries.shape.index(max(entries.shape))
    beside = spot[:main_axis] + [(spot[main_axis] + 1) % entries.shape[main_axis]] + spot[main_axis + 1:]
    return entries.at[tuple(spot)].set(low).at[tuple(beside)].set(top_value)


def block_levels(key, extent, cuts, low, largest):
    def one(axis_at, shards_of):
        draws = jax.random.uniform(jax.random.fold_in(jax.random.fold_in(key, 6), axis_at), (shards_of,), jnp.float32, low / len(cuts), largest / len(cuts))
        return jnp.repeat(jnp.exp(draws), extent[axis_at] // shards_of).reshape((-1,) + (1,) * (len(extent) - axis_at - 1))

    level = one(*cuts[0])
    for cut in cuts[1:]:
        level = level * one(*cut)
    return level


def length_profile(count, total, limit, slope):
    weights = [(1 << 20) // math.isqrt(rank ** slope) + 1 for rank in range(2, count + 1)]
    surplus, given = total - limit - (count - 1), [1] * (count - 1)
    while surplus > 0:
        candidates = [i for i in range(count - 1) if given[i] < limit]
        whole, left = sum([weights[i] for i in candidates]), surplus
        for i in candidates:
            extra = min(limit - given[i], max(1, left * weights[i] // whole), surplus)
            given[i] = given[i] + extra
            surplus = surplus - extra
    return np.array([limit] + given)


def ragged_sizes(key, number_of, total, limit, lean):
    if number_of == 2:
        one = jax.random.randint(key, (), max(1, total - limit), min(limit, total - 1) + 1)
        return jnp.stack([one, total - one])
    sizes = jnp.asarray(length_profile(number_of, total, limit, lean), jnp.int32)
    twos = (number_of - 1) // 2
    donor, receiver = sizes[1:1 + 2 * twos:2], sizes[2:2 + 2 * twos:2]
    margin = jnp.minimum(donor - 1, limit - receiver)
    passed = jax.random.randint(jax.random.fold_in(key, 1), (twos,), 0, 1 << 20) % (margin + 1)
    sizes = sizes.at[1:1 + 2 * twos:2].set(donor - passed).at[2:2 + 2 * twos:2].set(receiver + passed)
    return sizes[jax.random.permutation(jax.random.fold_in(key, 2), number_of)]


def setup_inputs(seed: int = 0, part: int = 0) -> dict:
    key_list = jax.random.split(jax.random.key(seed), 9)
    own_keys = jax.random.split(jax.random.fold_in(key_list[8], part), 9)
    return {
        "path_links": draw_path_links(jax.random.fold_in(jax.random.fold_in(key_list[8], part), 71), part),
        "block_tiles": draw_block_tiles(jax.random.fold_in(jax.random.fold_in(key_list[8], part), 71), part),
        "block_count": draw_block_count(jax.random.fold_in(jax.random.fold_in(key_list[8], part), 71), part),
        "path_commodity": jax.vmap(lambda own: jnp.searchsorted(jnp.cumsum(ragged_sizes(own, COMMODITY_BLOCK, PATHS_PER_BLOCK, 2 * PATHS_PER_BLOCK // COMMODITY_BLOCK, 1)), jnp.arange(PATHS_PER_BLOCK), side="right"))(jax.random.split(own_keys[3], BLOCK_TOTAL)).reshape((BLOCK_TOTAL, PATHS_PER_BLOCK)).astype(jnp.int32),
        "demand": touch_ends(jax.random.randint(own_keys[4], (S, COMM), 1, 65), jax.random.fold_in(own_keys[4], 1), 1, 64).astype(jnp.int32),
        "lengths": draw_lengths(jax.random.fold_in(jax.random.fold_in(key_list[8], part), 71), part),
        "capacity": jnp.clip(jnp.exp(math.log(32.0) - 2.0794415 * jax.random.uniform(own_keys[6], (L,), jnp.float32) ** block_levels(own_keys[6], (L,), ((0, 4),), -0.2, 0.2)), 4.0, 32.0),
        "scenario_weight": jnp.clip(jnp.exp(math.log(2.0) - 1.3862944 * jax.random.uniform(own_keys[7], (S,), jnp.float32) ** block_levels(own_keys[7], (S,), ((0, 4),), -0.2, 0.2)), 0.5, 2.0),
    }


SOFTMIN_RATE = 0.25
STEP_RATE = 1.0
DEMAND_UNIT = 0.0625
PRECISE = lax.Precision.HIGHEST


def incidence(hop_links, tile_ids, live_count):
    link_block = hop_links // LB
    column = hop_links % LB
    live_slots = jnp.arange(MAXT) < live_count
    slot_match = ((link_block[:, :, None] == tile_ids[None, None, :]) & live_slots[None, None, :]).astype(jnp.float32)
    column_hot = (column[:, :, None] == jnp.arange(LB)[None, None, :]).astype(jnp.float32)
    return jnp.einsum("hpt,hpl->ptl", slot_match, column_hot, precision=PRECISE)


def tile_costs(table_grid, tile_ids, tile_hits):
    chosen = jnp.take(table_grid, tile_ids, axis=1)
    return jnp.einsum("stl,ptl->sp", chosen, tile_hits, precision=PRECISE)


def tile_loads(block_flow, tile_hits):
    return jnp.einsum("sp,ptl->stl", block_flow, tile_hits, precision=PRECISE)


def block_flows(block_cost, commodity_id, block_demand):
    commodity_onehot = (commodity_id[:, None] == jnp.arange(COMMODITY_BLOCK)[None, :]).astype(jnp.float32)
    weight = jnp.exp(-SOFTMIN_RATE * block_cost)
    totals = jnp.dot(weight, commodity_onehot, preferred_element_type=jnp.float32, precision=PRECISE)
    per_path = jnp.dot(totals, commodity_onehot.T, preferred_element_type=jnp.float32, precision=PRECISE)
    wanted = jnp.dot(block_demand.astype(jnp.float32) * DEMAND_UNIT, commodity_onehot.T, preferred_element_type=jnp.float32, precision=PRECISE)
    return wanted * weight / per_path


def reference(path_links, block_tiles, block_count, path_commodity, demand, lengths, capacity, scenario_weight):
    block_list = block_tiles.shape[0]
    scenario_rows = lengths.shape[0]
    links_by_block = path_links.reshape(HOPS, block_list, PATHS_PER_BLOCK).transpose(1, 0, 2)
    block_demands = demand.reshape(scenario_rows, block_list, COMMODITY_BLOCK).transpose(1, 0, 2)
    length_grid = lengths.reshape(scenario_rows, -1, LB)

    def first_pass(load_grid, pieces):
        hop_links, tile_ids, live_count, commodity_id, block_demand = pieces
        tile_hits = incidence(hop_links, tile_ids, live_count)
        block_flow = block_flows(tile_costs(length_grid, tile_ids, tile_hits), commodity_id, block_demand)
        load_grid = load_grid.at[:, tile_ids, :].add(tile_loads(block_flow, tile_hits))
        return load_grid, block_flow

    load_grid, flow_blocks = lax.scan(first_pass, jnp.zeros(length_grid.shape, jnp.float32), (links_by_block, block_tiles, block_count, path_commodity, block_demands))
    flows = flow_blocks.transpose(1, 0, 2).reshape(scenario_rows, block_list * PATHS_PER_BLOCK)
    load_full = load_grid.reshape(scenario_rows, -1)
    grown_len = lengths * jnp.exp(STEP_RATE * load_full / capacity[None, :])
    lengths_next = grown_len * (lengths.shape[1] / jnp.sum(grown_len, axis=1))[:, None]
    next_grid = lengths_next.reshape(scenario_rows, -1, LB)

    def second_pass(carried, pieces):
        hop_links, tile_ids, live_count = pieces
        tile_hits = incidence(hop_links, tile_ids, live_count)
        block_cost = tile_costs(next_grid, tile_ids, tile_hits)
        mixed = jnp.dot(scenario_weight[None, :], block_cost, preferred_element_type=jnp.float32, precision=PRECISE)[0] / S
        return carried, mixed

    _, robust = lax.scan(second_pass, jnp.zeros((), jnp.float32), (links_by_block, block_tiles, block_count))
    return flows, lengths_next, robust.reshape(-1)
```

```python
import jax
import jax.numpy as jnp
from jax import lax
from jax.experimental import pallas as pl
from jax.experimental.pallas import tpu as pltpu
from jax.sharding import PartitionSpec as P

PATHS_PER_BLOCK = 128
LB = 128
MAXT = 16
COMMODITY_BLOCK = 32
S = 256
GROUP = LB // COMMODITY_BLOCK

SOFTMIN_RATE = 0.25
STEP_RATE = 1.0
DEMAND_UNIT = 0.0625
VMEM_BYTES = 56 * 1024 * 1024

F32 = jnp.float32
BF16 = jnp.bfloat16


def split(x):
    high = x.astype(BF16)
    return high, (x - high.astype(F32)).astype(BF16)


def whole(shape):
    return pl.BlockSpec(shape, lambda *_: (0,) * len(shape))


SCALARS = pl.BlockSpec(memory_space=pltpu.SMEM)


def incidence_kernel(tiles_ref, count_ref, links_ref, comm_ref, demand_ref, hits_ref, same_ref, wanted_ref):
    step = pl.program_id(0)
    pack = 16
    lane_rows = [
        (lax.broadcasted_iota(jnp.int32, (pack, LB), 0) + pack * g).astype(F32).astype(BF16) for g in range(LB // pack)
    ]
    demand = demand_ref[...].astype(F32).astype(BF16)
    commodity_rows = lax.broadcasted_iota(jnp.int32, (LB, PATHS_PER_BLOCK), 0)
    for j in range(GROUP):
        block = step * GROUP + j
        links = links_ref[:, j * PATHS_PER_BLOCK : (j + 1) * PATHS_PER_BLOCK]
        live = count_ref[block]
        commodity = comm_ref[pl.ds(block, 1), :] + COMMODITY_BLOCK * j
        onehot = (commodity_rows == commodity).astype(F32).astype(BF16)
        same = lax.dot_general(onehot, onehot, (((0,), (0,)), ((), ())), preferred_element_type=F32)
        same_ref[j] = same.astype(BF16)
        wanted = jnp.dot(demand, onehot, preferred_element_type=F32)
        wanted_ref[:, j * PATHS_PER_BLOCK : (j + 1) * PATHS_PER_BLOCK] = wanted * DEMAND_UNIT

        def one_slot(t, carry, j=j, block=block, links=links, live=live):
            start = pl.multiple_of(t * LB, LB)

            @pl.when(t < live)
            def _():
                place = (links - tiles_ref[block, t] * LB).astype(F32)
                totals = [jnp.zeros((pack, PATHS_PER_BLOCK), BF16) for _ in lane_rows]
                for h in range(links.shape[0]):
                    row = jnp.broadcast_to(place[h : h + 1, :], (pack, PATHS_PER_BLOCK)).astype(BF16)
                    totals = [
                        a + jnp.where(row == lane, jnp.ones_like(a), jnp.zeros_like(a))
                        for a, lane in zip(totals, lane_rows)
                    ]
                for g, a in enumerate(totals):
                    hits_ref[j, pl.ds(start + g * pack, pack), :] = a

            @pl.when(t >= live)
            def _():
                hits_ref[j, pl.ds(start, LB), :] = jnp.zeros((LB, PATHS_PER_BLOCK), BF16)

            return carry

        lax.fori_loop(0, MAXT, one_slot, 0)


def build_incidence(path_links, block_tiles, block_count, path_commodity, demand):
    hops, paths = path_links.shape
    blocks = block_tiles.shape[0]
    rows = demand.shape[0]
    wide = GROUP * PATHS_PER_BLOCK
    return pl.pallas_call(
        incidence_kernel,
        grid=(blocks // GROUP,),
        in_specs=[
            SCALARS,
            SCALARS,
            pl.BlockSpec((hops, wide), lambda i: (0, i)),
            whole(path_commodity.shape),
            pl.BlockSpec((rows, LB), lambda i: (0, i)),
        ],
        out_specs=[
            pl.BlockSpec((GROUP, MAXT * LB, PATHS_PER_BLOCK), lambda i: (i, 0, 0)),
            pl.BlockSpec((GROUP, PATHS_PER_BLOCK, PATHS_PER_BLOCK), lambda i: (i, 0, 0)),
            pl.BlockSpec((rows, wide), lambda i: (0, i)),
        ],
        out_shape=[
            jax.ShapeDtypeStruct((blocks, MAXT * LB, PATHS_PER_BLOCK), BF16),
            jax.ShapeDtypeStruct((blocks, PATHS_PER_BLOCK, PATHS_PER_BLOCK), BF16),
            jax.ShapeDtypeStruct((rows, paths), F32),
        ],
        compiler_params=pltpu.CompilerParams(vmem_limit_bytes=VMEM_BYTES),
        cost_estimate=pl.CostEstimate(flops=10**9, bytes_accessed=10**7, transcendentals=0),
        name="incidence",
    )(block_tiles, block_count, path_links, path_commodity, demand)


def flow_kernel(pieces, chunks, origin_ref, tiles_ref, *refs):
    piece_refs, (hits_ref, same_ref, wanted_ref) = refs[:pieces], refs[pieces : pieces + 3]
    flows_ref, *out_refs = refs[pieces + 3 : -2]
    split_ref, load_ref = refs[-2:]
    step = pl.program_id(0)
    tile_total, rows2, _ = split_ref.shape
    rows = rows2 // 2
    shard_tiles = piece_refs[0].shape[-1] // LB
    shards = [(i, r, s) for i, r in enumerate(piece_refs) for s in range(r.shape[0])]

    @pl.when(step == 0)
    def _():
        for i, ref, s in shards:
            first = (origin_ref[i] + s) * shard_tiles
            for k in range(shard_tiles):
                high, low = split(ref[s, :, k * LB : (k + 1) * LB])
                split_ref[first + k, :rows, :] = high
                split_ref[first + k, rows:, :] = low
        load_ref[...] = jnp.zeros_like(load_ref)

    for j in range(GROUP):
        block = step * GROUP + j
        ids = [tiles_ref[block, t] for t in range(MAXT)]
        chosen = jnp.concatenate([split_ref[i] for i in ids], axis=1)
        cost = jnp.dot(chosen, hits_ref[j], preferred_element_type=F32)
        cost = cost[:rows] + cost[rows:]
        weight = jnp.exp(-SOFTMIN_RATE * cost)
        high, low = split(weight)
        total = jnp.dot(jnp.concatenate([high, low], axis=0), same_ref[j], preferred_element_type=F32)
        total = total[:rows] + total[rows:]
        columns = slice(j * PATHS_PER_BLOCK, (j + 1) * PATHS_PER_BLOCK)
        flow = wanted_ref[:, columns] * weight / total
        flows_ref[:, columns] = flow
        high, low = split(flow)
        load = lax.dot_general(
            jnp.concatenate([high, low], axis=0), hits_ref[j], (((1,), (1,)), ((), ())), preferred_element_type=F32
        )
        for t, i in enumerate(ids):
            load_ref[i] += load[:, t * LB : (t + 1) * LB]

    @pl.when(step == pl.num_programs(0) - 1)
    def _():
        if not chunks:
            for k in range(tile_total):
                out_refs[0][:, k * LB : (k + 1) * LB] = load_ref[k, :rows, :] + load_ref[k, rows:, :]
            return
        height = rows // chunks
        for d in range(chunks):
            row = pl.multiple_of(lax.rem(origin_ref[0] + d, chunks) * height, height)
            for k in range(tile_total):
                out_refs[d][:, k * LB : (k + 1) * LB] = (
                    load_ref[k, pl.ds(row, height), :] + load_ref[k, pl.ds(rows + row, height), :]
                )
        row = pl.multiple_of(origin_ref[0] * height, height)
        for i, ref, s in shards:
            first = (origin_ref[i] + s) * shard_tiles
            for k in range(shard_tiles):
                out_refs[chunks][:, pl.ds(pl.multiple_of((first + k) * LB, LB), LB)] = ref[
                    s, pl.ds(row, height), k * LB : (k + 1) * LB
                ]


def flows_and_loads(pieces, origin, block_tiles, hits, same, wanted, chunks):
    blocks = block_tiles.shape[0]
    _, rows, own = pieces[0].shape
    paths = wanted.shape[1]
    links = own * sum(p.shape[0] for p in pieces)
    wide = GROUP * PATHS_PER_BLOCK
    outs = [(rows // chunks, links)] * (chunks + 1) if chunks else [(rows, links)]
    return pl.pallas_call(
        lambda *refs: flow_kernel(len(pieces), chunks, *refs),
        grid=(blocks // GROUP,),
        in_specs=[SCALARS, SCALARS]
        + [whole(p.shape) for p in pieces]
        + [
            pl.BlockSpec((GROUP, MAXT * LB, PATHS_PER_BLOCK), lambda i: (i, 0, 0)),
            pl.BlockSpec((GROUP, PATHS_PER_BLOCK, PATHS_PER_BLOCK), lambda i: (i, 0, 0)),
            pl.BlockSpec((rows, wide), lambda i: (0, i)),
        ],
        out_specs=[pl.BlockSpec((rows, wide), lambda i: (0, i))] + [whole(o) for o in outs],
        out_shape=[jax.ShapeDtypeStruct((rows, paths), F32)] + [jax.ShapeDtypeStruct(o, F32) for o in outs],
        scratch_shapes=[
            pltpu.VMEM((links // LB, 2 * rows, LB), BF16),
            pltpu.VMEM((links // LB, 2 * rows, LB), F32),
        ],
        compiler_params=pltpu.CompilerParams(vmem_limit_bytes=VMEM_BYTES),
        cost_estimate=pl.CostEstimate(flops=10**10, bytes_accessed=10**7, transcendentals=10**5),
        name="flows",
    )(origin, block_tiles, *pieces, hits, same, wanted)


def growth_kernel(chunks, me_ref, *refs):
    load_refs, (length_ref, weight_ref) = refs[:chunks], refs[chunks : chunks + 2]
    capacity_refs = refs[chunks + 2 : 2 * chunks + 2]
    next_refs, mixed_ref = refs[2 * chunks + 2 : 3 * chunks + 2], refs[-2]
    grown_ref = refs[-1]
    me = me_ref[0]
    height, links = length_ref.shape
    shard = links // chunks
    tiles = shard // LB
    total = jnp.zeros((height, LB), F32)
    for d in range(chunks):
        first = lax.rem(me + chunks - d, chunks)
        for k in range(tiles):
            place = pl.ds(pl.multiple_of((first * tiles + k) * LB, LB), LB)
            load = load_refs[0][:, place]
            for ref in load_refs[1:]:
                load = load + ref[:, place]
            grown = length_ref[:, place] * jnp.exp(STEP_RATE * load / capacity_refs[d][:, k * LB : (k + 1) * LB])
            grown_ref[first * tiles + k] = grown
            total = total + grown
    factor = links / jnp.sum(total, axis=1, keepdims=True)
    weight = weight_ref[pl.ds(pl.multiple_of(me * height, height), height), :]
    for d in range(chunks):
        first = lax.rem(me + d, chunks)
        for k in range(tiles):
            new = grown_ref[first * tiles + k] * factor
            next_refs[d][:, k * LB : (k + 1) * LB] = new
            mixed_ref[pl.ds(first * tiles + k, 1), :] = jnp.sum(weight * new, axis=0, keepdims=True)


def grow(me, loads, lengths, weights, capacities):
    chunks = len(loads)
    height, links = lengths.shape
    out = [jax.ShapeDtypeStruct((height, links // chunks), F32)] * chunks + [jax.ShapeDtypeStruct((links // LB, LB), F32)]
    vmem = pl.BlockSpec(memory_space=pltpu.VMEM)
    return pl.pallas_call(
        lambda *refs: growth_kernel(chunks, *refs),
        in_specs=[SCALARS] + [vmem] * (2 * chunks + 2),
        out_specs=[vmem] * (chunks + 1),
        out_shape=out,
        scratch_shapes=[pltpu.VMEM((links // LB, height, LB), F32)],
        compiler_params=pltpu.CompilerParams(vmem_limit_bytes=VMEM_BYTES),
        name="growth",
    )(me, *loads, lengths, weights, *capacities)


def robust_kernel(parts, tiles_ref, *refs):
    part_refs, hits_ref, out_ref, mixed_ref = refs[:parts], refs[parts], refs[-2], refs[-1]
    step = pl.program_id(0)

    @pl.when(step == 0)
    def _():
        mixed = part_refs[0][...]
        for ref in part_refs[1:]:
            mixed = mixed + ref[...]
        high = mixed.astype(BF16)
        rest = mixed - high.astype(F32)
        middle = rest.astype(BF16)
        low = (rest - middle.astype(F32)).astype(BF16)
        for k in range(mixed.shape[0]):
            mixed_ref[k] = jnp.concatenate(
                [jnp.broadcast_to(v[k : k + 1].astype(F32), (8, LB)) for v in (high, middle, low)], axis=0
            ).astype(BF16)

    for j in range(GROUP):
        block = step * GROUP + j
        chosen = jnp.concatenate([mixed_ref[tiles_ref[block, t]] for t in range(MAXT)], axis=1)
        cost = jnp.dot(chosen, hits_ref[j], preferred_element_type=F32)
        out_ref[pl.ds(block, 1), :] = (cost[0:1] + cost[8:9] + cost[16:17]) / S


def robust_costs(block_tiles, parts, hits):
    blocks = block_tiles.shape[0]
    out = pl.pallas_call(
        lambda *refs: robust_kernel(len(parts), *refs),
        grid=(blocks // GROUP,),
        in_specs=[SCALARS]
        + [whole(p.shape) for p in parts]
        + [pl.BlockSpec((GROUP, MAXT * LB, PATHS_PER_BLOCK), lambda i: (i, 0, 0))],
        out_specs=whole((blocks, PATHS_PER_BLOCK)),
        out_shape=jax.ShapeDtypeStruct((blocks, PATHS_PER_BLOCK), F32),
        scratch_shapes=[pltpu.VMEM((parts[0].shape[0], 24, LB), BF16)],
        compiler_params=pltpu.CompilerParams(vmem_limit_bytes=VMEM_BYTES),
        name="robust",
    )(block_tiles, *parts, hits)
    return out.reshape(-1)


def exchange(x, axis, n, bit):
    return lax.ppermute(x, axis, [(i, i ^ bit) for i in range(n)])


def shift(x, axis, n, d):
    return lax.ppermute(x, axis, [(i, (i + d) % n) for i in range(n)])


def power_of_two(n):
    return n & (n - 1) == 0


def body_direct(sizes, path_links, block_tiles, block_count, path_commodity, demand, lengths, capacity, scenario_weight):
    n = sizes["path"]
    rows, own = lengths.shape
    index = lax.axis_index("path").astype(jnp.int32)
    origin = jnp.stack([lax.rem(index + n - d, n) for d in range(n)])
    pieces = [lengths] + [shift(lengths, "path", n, d) for d in range(1, n)]
    capacity_row = capacity[None, :]
    capacities = [capacity_row] + [shift(capacity_row, "path", n, d) for d in range(1, n)]
    hits, same, wanted = build_incidence(path_links, block_tiles, block_count, path_commodity, demand)
    flows, *chunks = flows_and_loads([p[None] for p in pieces], origin, block_tiles, hits, same, wanted, n)
    loads = [chunks[0]] + [shift(chunks[d], "path", n, d) for d in range(1, n)]
    *new, mixed = grow(origin, loads, chunks[n], scenario_weight[:, None], capacities)
    arrived = [new[0]] + [shift(new[d], "path", n, d) for d in range(1, n)]
    height = rows // n
    for axis in ("sub", "scen"):
        bit = 1
        while bit < sizes[axis]:
            mixed = mixed + exchange(mixed, axis, sizes[axis], bit)
            bit *= 2
    bit, parts = 1, [mixed]
    while bit < n:
        mixed = sum(parts[1:], parts[0])
        parts = [mixed, exchange(mixed, "path", n, bit)]
        bit *= 2
    robust = robust_costs(block_tiles, parts, hits)
    lengths_next = jnp.zeros((rows, own), F32)
    for d in range(n):
        lengths_next = lax.dynamic_update_slice(lengths_next, arrived[d], (origin[d] * height, 0))
    return flows, lengths_next, robust


def body_wide(sizes, path_links, block_tiles, block_count, path_commodity, demand, lengths, capacity, scenario_weight):
    gathered = lax.all_gather(lengths, "path", axis=0, tiled=False)
    hits, same, wanted = build_incidence(path_links, block_tiles, block_count, path_commodity, demand)
    origin = jnp.zeros((1,), jnp.int32)
    flows, loads = flows_and_loads([gathered], origin, block_tiles, hits, same, wanted, 0)
    own_loads = lax.psum_scatter(loads, "path", scatter_dimension=1, tiled=True)
    grown = lengths * jnp.exp(STEP_RATE * own_loads / capacity[None, :])
    totals = lax.psum(jnp.sum(grown, axis=1), "path")
    lengths_next = grown * (loads.shape[1] / totals)[:, None]
    mixed = lax.psum(jnp.sum(lengths_next * scenario_weight[:, None], axis=0), ("scen", "sub"))
    mixed = lax.all_gather(mixed.reshape(-1, LB), "path", axis=0, tiled=True)
    return flows, lengths_next, robust_costs(block_tiles, [mixed], hits)


def solution(mesh):
    sizes = dict(mesh.shape)

    def body(*args):
        n, rows = sizes["path"], args[5].shape[0]
        direct = n <= 8 and rows % (16 * n) == 0 and all(power_of_two(sizes[a]) for a in ("path", "scen", "sub"))
        return (body_direct if direct else body_wide)(sizes, *args)

    return jax.shard_map(
        body,
        mesh=mesh,
        in_specs=(
            P(None, ("grp", "path")),
            P(("grp", "path"), None),
            P(("grp", "path")),
            P(("grp", "path"), None),
            P(("scen", "sub"), ("grp", "path")),
            P(("scen", "sub"), ("grp", "path")),
            P(("grp", "path")),
            P(("grp", "scen", "sub")),
        ),
        out_specs=(
            P(("scen", "sub"), ("grp", "path")),
            P(("scen", "sub"), ("grp", "path")),
            P(("grp", "path")),
        ),
        check_vma=False,
    )
```

```python
import jax
import jax.numpy as jnp
from jax import lax
from jax.experimental import pallas as pl
from jax.experimental.pallas import tpu as pltpu
from jax.sharding import PartitionSpec as P

PATHS_PER_BLOCK = 128
LB = 128
MAXT = 16
COMMODITY_BLOCK = 32
S = 256

SOFTMIN_RATE = 0.25
STEP_RATE = 1.0
DEMAND_UNIT = 0.0625
MIB = 1024 * 1024

F32 = jnp.float32
BF16 = jnp.bfloat16
PACK = 16
BATCH = 16
GROUP = LB // COMMODITY_BLOCK

SCALARS = pl.BlockSpec(memory_space=pltpu.SMEM)
ARRAY = pl.BlockSpec(memory_space=pltpu.VMEM)
LISTS = 4


def split(x):
    high = x.astype(BF16)
    return high, (x - high.astype(F32)).astype(BF16)


def stacked(x):
    return jnp.concatenate(split(x), axis=0)


def aligned(start, size, unit):
    return pl.ds(pl.multiple_of(start * unit, unit), size)


def incidence_kernel(*refs):
    given, (hits_ref, turned_ref, list_ref, total_ref, same_ref, wanted_ref) = refs[:5], refs[5:11]
    local, arrived = refs[11:16], refs[16]
    copies = [pltpu.make_async_copy(a, b, arrived.at[i]) for i, (a, b) in enumerate(zip(given, local))]
    for copy in copies:
        copy.start()
    for copy in copies:
        copy.wait()
    tiles_ref, count_ref, links_ref, comm_ref, demand_ref = local
    blocks = tiles_ref.shape[0]
    lanes = [(lax.broadcasted_iota(jnp.int32, (PACK, LB), 0) + PACK * g).astype(F32).astype(BF16) for g in range(LB // PACK)]
    one, zero = jnp.ones((PACK, PATHS_PER_BLOCK), BF16), jnp.zeros((PACK, PATHS_PER_BLOCK), BF16)
    spare = blocks * MAXT

    for ref in (hits_ref, turned_ref):
        ref[spare * LB :, :] = jnp.zeros((2 * LB, LB), BF16)

    def one_block(block, entry):
        links = links_ref[:, aligned(block, PATHS_PER_BLOCK, PATHS_PER_BLOCK)]
        live = count_ref[block]

        def one_pair(pair, entry):
            slot = block * MAXT + 2 * pair
            list_ref[0, entry] = slot
            list_ref[1, entry] = block
            for side in range(2):
                tile = tiles_ref[block, 2 * pair + side]
                list_ref[2 + side, entry] = tile
                first = jnp.where(2 * pair + side < live, tile * LB, 1 << 20)
                place = (links - first).astype(F32)
                counts = None
                for h in range(links.shape[0]):
                    row = jnp.broadcast_to(place[h : h + 1, :], (PACK, PATHS_PER_BLOCK)).astype(BF16)
                    hit = [jnp.where(row == lane, one, zero) for lane in lanes]
                    counts = hit if counts is None else [a + b for a, b in zip(counts, hit)]
                table = jnp.concatenate(counts, axis=0)
                where = aligned(slot + side, LB, LB)
                hits_ref[where, :] = table
                turned_ref[where, :] = table.T
            return entry + 1

        return lax.fori_loop(0, (live + 1) // 2, one_pair, entry)

    entries = lax.fori_loop(0, blocks, one_block, 0)
    batches = (entries + BATCH - 1) // BATCH
    total_ref[0] = batches

    def pad(entry, carry):
        list_ref[0, entry] = spare
        for i in range(1, LISTS):
            list_ref[i, entry] = 0
        return carry

    lax.fori_loop(entries, batches * BATCH, pad, 0)

    commodity_rows = lax.broadcasted_iota(jnp.int32, (LB, PATHS_PER_BLOCK), 0)
    for block in range(blocks):
        group, j = block // GROUP, block % GROUP
        demand = demand_ref[:, group * LB : (group + 1) * LB].astype(F32).astype(BF16)
        onehot = (commodity_rows == comm_ref[block : block + 1, :] + COMMODITY_BLOCK * j).astype(F32).astype(BF16)
        same = lax.dot_general(onehot, onehot, (((0,), (0,)), ((), ())), preferred_element_type=F32)
        same_ref[block] = same.astype(BF16)
        wanted = jnp.dot(demand, onehot, preferred_element_type=F32)
        wanted_ref[block] = wanted * DEMAND_UNIT


def build_incidence(path_links, block_tiles, block_count, path_commodity, demand):
    blocks = block_tiles.shape[0]
    rows = demand.shape[0]
    slots = blocks * MAXT + 2
    given = (block_tiles, block_count, path_links, path_commodity, demand)
    given = tuple(pltpu.with_memory_space_constraint(a, pltpu.HBM) for a in given)
    return pl.pallas_call(
        incidence_kernel,
        in_specs=[pl.BlockSpec(memory_space=pltpu.HBM)] * 5,
        out_specs=[ARRAY, ARRAY, SCALARS, SCALARS, ARRAY, ARRAY],
        scratch_shapes=[pltpu.SMEM(a.shape, a.dtype) for a in given[:2]]
        + [pltpu.VMEM(a.shape, a.dtype) for a in given[2:]]
        + [pltpu.SemaphoreType.DMA((5,))],
        out_shape=[
            jax.ShapeDtypeStruct((slots * LB, PATHS_PER_BLOCK), BF16),
            jax.ShapeDtypeStruct((slots * PATHS_PER_BLOCK, LB), BF16),
            jax.ShapeDtypeStruct((LISTS, blocks * MAXT // 2 + BATCH), jnp.int32),
            jax.ShapeDtypeStruct((1,), jnp.int32),
            jax.ShapeDtypeStruct((blocks, PATHS_PER_BLOCK, PATHS_PER_BLOCK), BF16),
            jax.ShapeDtypeStruct((blocks, rows, PATHS_PER_BLOCK), F32),
        ],
        compiler_params=pltpu.CompilerParams(vmem_limit_bytes=8 * MIB),
        cost_estimate=pl.CostEstimate(flops=10**9, bytes_accessed=25 * 10**6, transcendentals=0),
        name="incidence",
    )(*given)


def sweep(list_ref, total_ref, hits_ref, turned_ref, same_ref, wanted_at, put_flow, split_ref, cost_ref, flow_ref, load_ref):
    blocks, rows2, _ = cost_ref.shape
    rows = rows2 // 2
    load_ref[...] = jnp.zeros_like(load_ref)
    cost_ref[...] = jnp.zeros_like(cost_ref)
    batches = total_ref[0]

    def cost_batch(batch, carry):
        done = []
        for j in range(BATCH):
            slot, block, left, right = (list_ref[i, batch * BATCH + j] for i in range(LISTS))
            chosen = jnp.concatenate([split_ref[left], split_ref[right]], axis=1)
            done.append((block, jnp.dot(chosen, hits_ref[aligned(slot, 2 * LB, LB), :], preferred_element_type=F32)))
        for block, cost in done:
            cost_ref[block] += cost
        return carry

    lax.fori_loop(0, batches, cost_batch, 0)

    for block in range(blocks):
        weight = jnp.exp(-SOFTMIN_RATE * (cost_ref[block, :rows] + cost_ref[block, rows:]))
        total = jnp.dot(stacked(weight), same_ref[block], preferred_element_type=F32)
        flow = wanted_at(block) * weight / (total[:rows] + total[rows:])
        put_flow(block, flow)
        flow_ref[block] = stacked(flow)

    def load_batch(batch, carry):
        done = []
        for j in range(BATCH):
            slot, block, left, right = (list_ref[i, batch * BATCH + j] for i in range(LISTS))
            for side, tile in enumerate((left, right)):
                turned = turned_ref[aligned(slot + side, LB, LB), :]
                done.append((tile, jnp.dot(flow_ref[block], turned, preferred_element_type=F32)))
        for tile, load in done:
            load_ref[tile] += load
        return carry

    lax.fori_loop(0, batches, load_batch, 0)


def spread(split_ref, first, shard):
    for k in range(shard.shape[-1] // LB):
        split_ref[first + k] = stacked(shard[:, k * LB : (k + 1) * LB])


def path_columns(block):
    return slice(block * PATHS_PER_BLOCK, (block + 1) * PATHS_PER_BLOCK)


def sweep_scratch(rows, tiles, blocks):
    return [
        pltpu.VMEM((tiles, 2 * rows, LB), BF16),
        pltpu.VMEM((blocks, 2 * rows, PATHS_PER_BLOCK), F32),
        pltpu.VMEM((blocks, 2 * rows, PATHS_PER_BLOCK), BF16),
        pltpu.VMEM((tiles, 2 * rows, LB), F32),
    ]


SWEEP_COST = pl.CostEstimate(flops=10**9, bytes_accessed=25 * 10**6, transcendentals=10**5)


def half_kernel(far, n, list_ref, total_ref, *refs):
    pieces, (hits_ref, turned_ref, same_ref, wanted_ref) = refs[:n], refs[n : n + 4]
    flows_ref, mine_ref, other_ref, *scratch = refs[-7:]
    z = lax.axis_index("path")
    rows = scratch[0].shape[1] // 2
    side = lax.div(z, 2)
    side = 1 - side if far else side
    shard_tiles = pieces[0].shape[1] // LB
    for m, piece in enumerate(pieces):
        start = side if piece.shape[0] == 2 * rows else 0
        spread(scratch[0], (z ^ m) * shard_tiles, piece[aligned(start, rows, rows), :])

    def wanted_at(block):
        return wanted_ref[block, aligned(side, rows, rows), :]

    def put_flow(block, flow):
        if far:
            flows_ref[:, path_columns(block)] = flow
        else:
            flows_ref[aligned(side, rows, rows), path_columns(block)] = flow

    if not far:
        flows_ref[aligned(1 - side, rows, rows), :] = refs[n + 4][...]
    sweep(list_ref, total_ref, hits_ref, turned_ref, same_ref, wanted_at, put_flow, *scratch)
    load_ref = scratch[3]
    height = rows // 2
    for out_ref, place in ((mine_ref, lax.rem(z, 2)), (other_ref, 1 - lax.rem(z, 2))):
        for k in range(load_ref.shape[0]):
            high = load_ref[k, aligned(place, height, height), :]
            out_ref[k] = high + load_ref[k, pl.ds(pl.multiple_of(rows + place * height, height), height), :]


def half_sweep(pieces, rows, built, far_flows=None):
    hits, turned, pairs, total, same, wanted = built
    own = pieces[0].shape[1]
    n = len(pieces)
    blocks = wanted.shape[0]
    tiles = n * own // LB
    far = far_flows is None
    extra = [] if far else [far_flows]
    return pl.pallas_call(
        lambda *refs: half_kernel(far, n, *refs),
        in_specs=[SCALARS, SCALARS] + [ARRAY] * (n + 4 + len(extra)),
        out_specs=[ARRAY] * 3,
        out_shape=[jax.ShapeDtypeStruct((rows if far else 2 * rows, blocks * PATHS_PER_BLOCK), F32)]
        + [jax.ShapeDtypeStruct((tiles, rows // 2, LB), F32)] * 2,
        scratch_shapes=sweep_scratch(rows, tiles, blocks),
        compiler_params=pltpu.CompilerParams(vmem_limit_bytes=16 * MIB),
        cost_estimate=SWEEP_COST,
        name="far_sweep" if far else "near_sweep",
    )(pairs, total, *pieces, hits, turned, same, wanted, *extra)


def wide_kernel(list_ref, total_ref, lengths_ref, hits_ref, turned_ref, same_ref, wanted_ref, flows_ref, out_ref, *scratch):
    shards, _, own = lengths_ref.shape
    rows = lengths_ref.shape[1]

    def one_shard(i, carry):
        spread(scratch[0], i * (own // LB), lengths_ref[i])
        return carry

    lax.fori_loop(0, shards, one_shard, 0)

    def put_flow(block, flow):
        flows_ref[:, path_columns(block)] = flow

    sweep(
        list_ref, total_ref, hits_ref, turned_ref, same_ref, lambda block: wanted_ref[block], put_flow, *scratch
    )
    out_ref[...] = scratch[3][:, :rows, :] + scratch[3][:, rows:, :]


def wide_sweep(lengths, built):
    hits, turned, pairs, total, same, wanted = built
    shards, rows, own = lengths.shape
    blocks = wanted.shape[0]
    tiles = shards * own // LB
    return pl.pallas_call(
        wide_kernel,
        in_specs=[SCALARS, SCALARS] + [ARRAY] * 5,
        out_specs=[ARRAY] * 2,
        out_shape=[
            jax.ShapeDtypeStruct((rows, blocks * PATHS_PER_BLOCK), F32),
            jax.ShapeDtypeStruct((tiles, rows, LB), F32),
        ],
        scratch_shapes=sweep_scratch(rows, tiles, blocks),
        compiler_params=pltpu.CompilerParams(vmem_limit_bytes=48 * MIB),
        cost_estimate=SWEEP_COST,
        name="wide_sweep",
    )(pairs, total, lengths, hits, turned, same, wanted)


def growth_kernel(n, parts, *refs):
    lengths, capacities, weight_ref = refs[:n], refs[n : 2 * n], refs[2 * n]
    loads = refs[2 * n + 1 : 2 * n + 1 + parts]
    next_refs, mixed_ref, grown_ref = refs[-n - 2 : -2], refs[-2], refs[-1]
    z = lax.axis_index("path")
    links_total, height, _ = grown_ref.shape
    shard_tiles = links_total // n
    total = jnp.zeros((height, LB), F32)
    for m in range(n):
        row = aligned(z if lengths[m].shape[0] == n * height else lax.rem(z, 2), height, height)
        first = (z ^ m) * shard_tiles
        for k in range(shard_tiles):
            columns = slice(k * LB, (k + 1) * LB)
            load = loads[0][first + k]
            for ref in loads[1:]:
                load = load + ref[first + k]
            grown = lengths[m][row, columns] * jnp.exp(STEP_RATE * load / capacities[m][-1:, columns])
            grown_ref[m * shard_tiles + k] = grown
            total = total + grown
    factor = (links_total * LB) / jnp.sum(total, axis=1, keepdims=True)
    weight = weight_ref[aligned(z, height, height), :]
    for m in range(n):
        first = (z ^ m) * shard_tiles
        for k in range(shard_tiles):
            new = grown_ref[m * shard_tiles + k] * factor
            next_refs[m][:, k * LB : (k + 1) * LB] = new
            mixed_ref[pl.ds(first + k, 1), :] = jnp.sum(weight * new, axis=0, keepdims=True)


def grow(loads, lengths, capacities, weights):
    n, parts = len(lengths), len(loads)
    tiles, height, _ = loads[0].shape
    return pl.pallas_call(
        lambda *refs: growth_kernel(n, parts, *refs),
        in_specs=[ARRAY] * (2 * n + 1 + parts),
        out_specs=[ARRAY] * (n + 1),
        out_shape=[jax.ShapeDtypeStruct((height, tiles * LB // n), F32)] * n + [jax.ShapeDtypeStruct((tiles, LB), F32)],
        scratch_shapes=[pltpu.VMEM((tiles, height, LB), F32)],
        compiler_params=pltpu.CompilerParams(vmem_limit_bytes=8 * MIB),
        cost_estimate=pl.CostEstimate(flops=10**6, bytes_accessed=5 * 10**6, transcendentals=10**5),
        name="growth",
    )(*lengths, *capacities, weights, *loads)


def robust_kernel(parts, list_ref, total_ref, links_ref, *refs):
    part_refs, (out_ref, mixed_ref, cost_ref) = refs[:parts], refs[parts:]
    blocks = out_ref.shape[0]
    mixed = part_refs[0][...]
    for ref in part_refs[1:]:
        mixed = mixed + ref[...]
    mixed_ref[...] = mixed
    cost_ref[...] = jnp.zeros_like(cost_ref)
    spare = blocks * MAXT

    def batch_step(batch, carry):
        done = []
        for j in range(BATCH):
            slot, block, left, right = (list_ref[i, batch * BATCH + j] for i in range(LISTS))
            links = links_ref[:, aligned(block, PATHS_PER_BLOCK, PATHS_PER_BLOCK)]
            for tile in (left, right):
                place = links - jnp.where(slot < spare, tile * LB, 1 << 20)
                table = jnp.broadcast_to(mixed_ref[pl.ds(tile, 1), :], links.shape)
                found = jnp.take_along_axis(table, place & (LB - 1), axis=1)
                done.append((block, jnp.where((place >= 0) & (place < LB), found, 0.0)))
        for block, cost in done:
            cost_ref[block] += cost
        return carry

    lax.fori_loop(0, total_ref[0], batch_step, 0)
    for block in range(blocks):
        out_ref[block : block + 1, :] = jnp.sum(cost_ref[block], axis=0, keepdims=True) / S


def robust_costs(path_links, built, parts):
    _, _, pairs, total, _, wanted = built
    blocks = wanted.shape[0]
    hops = path_links.shape[0]
    out = pl.pallas_call(
        lambda *refs: robust_kernel(len(parts), *refs),
        in_specs=[SCALARS, SCALARS] + [ARRAY] * (len(parts) + 1),
        out_specs=ARRAY,
        out_shape=jax.ShapeDtypeStruct((blocks, PATHS_PER_BLOCK), F32),
        scratch_shapes=[pltpu.VMEM(parts[0].shape, F32), pltpu.VMEM((blocks, hops, PATHS_PER_BLOCK), F32)],
        compiler_params=pltpu.CompilerParams(vmem_limit_bytes=8 * MIB),
        cost_estimate=pl.CostEstimate(flops=10**8, bytes_accessed=10**7, transcendentals=0),
        name="robust",
    )(pairs, total, path_links, *parts)
    return out.reshape(-1)


def exchange(x, axis, n, bit):
    return lax.ppermute(x, axis, [(i, i ^ bit) for i in range(n)])


def body_paired(sizes, path_links, block_tiles, block_count, path_commodity, demand, lengths, capacity, scenario_weight):
    n = sizes["path"]
    rows, own = lengths.shape
    half, height = rows // 2, rows // n
    z = lax.axis_index("path").astype(jnp.int32)
    side = z // 2
    far = lax.dynamic_slice(lengths, ((1 - side) * half, 0), (half, own))
    far = jnp.concatenate([far, jnp.broadcast_to(capacity[None, :], (8, own))], axis=0)
    near = lax.dynamic_slice(lengths, (side * half, 0), (half, own))

    def swap(x, m):
        return exchange(x, "path", n, m)

    shared = swap(lengths, 1)
    far_pieces = [lengths, shared, swap(near, 2), swap(near, 3)]
    near_pieces = [lengths, shared, swap(far, 2), swap(far, 3)]
    built = build_incidence(path_links, block_tiles, block_count, path_commodity, demand)
    far_flows, straight, crossed = half_sweep(far_pieces, half, built)
    partial = straight + swap(crossed, 1)
    flows, mine, other = half_sweep(near_pieces, half, built, far_flows)
    loads = [mine, swap(other, 1), swap(partial, 2)]
    capacity_row = capacity[None, :]
    capacities = [capacity_row, swap(capacity_row, 1), near_pieces[2], near_pieces[3]]
    *new, mixed = grow(loads, near_pieces, capacities, scenario_weight[:, None])
    mixed = mixed + exchange(mixed, "sub", 2, 1)
    mixed = mixed + exchange(mixed, "scen", 2, 1)
    mixed = mixed + swap(mixed, 1)
    parts = [mixed, swap(mixed, 2)]
    arrived = [new[0]] + [swap(new[m], m) for m in range(1, n)]
    robust = robust_costs(path_links, built, parts)
    lengths_next = jnp.zeros((rows, own), F32)
    for m in range(n):
        lengths_next = lax.dynamic_update_slice(lengths_next, arrived[m], ((z ^ m) * height, 0))
    return flows, lengths_next, robust


def body_wide(sizes, path_links, block_tiles, block_count, path_commodity, demand, lengths, capacity, scenario_weight):
    gathered = lax.all_gather(lengths, "path", axis=0, tiled=False)
    built = build_incidence(path_links, block_tiles, block_count, path_commodity, demand)
    flows, loads = wide_sweep(gathered, built)
    loads = loads.transpose(1, 0, 2).reshape(lengths.shape[0], -1)
    own_loads = lax.psum_scatter(loads, "path", scatter_dimension=1, tiled=True)
    grown = lengths * jnp.exp(STEP_RATE * own_loads / capacity[None, :])
    totals = lax.psum(jnp.sum(grown, axis=1), "path")
    lengths_next = grown * (loads.shape[1] / totals)[:, None]
    mixed = lax.psum(jnp.sum(lengths_next * scenario_weight[:, None], axis=0), ("scen", "sub"))
    mixed = lax.all_gather(mixed.reshape(-1, LB), "path", axis=0, tiled=True)
    return flows, lengths_next, robust_costs(path_links, built, [mixed])


def solution(mesh):
    sizes = dict(mesh.shape)

    def body(*args):
        paired = sizes["path"] == 4 and sizes["scen"] == 2 and sizes["sub"] == 2 and args[5].shape[0] % 64 == 0
        return (body_paired if paired else body_wide)(sizes, *args)

    return jax.shard_map(
        body,
        mesh=mesh,
        in_specs=(
            P(None, ("grp", "path")),
            P(("grp", "path"), None),
            P(("grp", "path")),
            P(("grp", "path"), None),
            P(("scen", "sub"), ("grp", "path")),
            P(("scen", "sub"), ("grp", "path")),
            P(("grp", "path")),
            P(("grp", "scen", "sub")),
        ),
        out_specs=(
            P(("scen", "sub"), ("grp", "path")),
            P(("scen", "sub"), ("grp", "path")),
            P(("grp", "path")),
        ),
        check_vma=False,
    )
```

```python
import jax
import jax.numpy as jnp
from jax import lax
from jax.experimental import pallas as pl
from jax.experimental.pallas import tpu as pltpu
from jax.sharding import PartitionSpec as P

PATHS_PER_BLOCK = 128
LB = 128
MAXT = 16
COMMODITY_BLOCK = 32
S = 256

SOFTMIN_RATE = 0.25
STEP_RATE = 1.0
DEMAND_UNIT = 0.0625
MIB = 1024 * 1024

F32 = jnp.float32
BF16 = jnp.bfloat16
PACK = 16
BATCH = 16
GROUP = LB // COMMODITY_BLOCK

SCALARS = pl.BlockSpec(memory_space=pltpu.SMEM)
ARRAY = pl.BlockSpec(memory_space=pltpu.VMEM)
LISTS = 3
TOGETHER = 8
UNROLL = 7
LB_BITS = 7
COUNTED = 8


def split(x):
    high = x.astype(BF16)
    return high, (x - high.astype(F32)).astype(BF16)


def stacked(x):
    return jnp.concatenate(split(x), axis=0)


def aligned(start, size, unit):
    return pl.ds(pl.multiple_of(start * unit, unit), size)


def stay(*arrays):
    return tuple(pltpu.with_memory_space_constraint(a, pltpu.HBM) for a in arrays)


REMAIN = pl.BlockSpec(memory_space=pltpu.HBM)


def fetch(given, local, arrived):
    copies = [pltpu.make_async_copy(a, b, arrived.at[i]) for i, (a, b) in enumerate(zip(given, local))]
    for copy in copies:
        copy.start()
    return copies


def listing_kernel(tile_total, *refs):
    given, (list_ref, total_ref, same_ref, wanted_ref) = refs[:4], refs[4:8]
    local, arrived = refs[8:12], refs[12]
    tiles_ref, count_ref, comm_ref, demand_ref = local
    copies = fetch(given, local, arrived)
    blocks = tiles_ref.shape[0]
    spare = blocks * MAXT
    for copy in copies:
        copy.wait()

    def one_block(block, entry):
        live = count_ref[block]

        def one_pair(pair, entry):
            list_ref[0, entry] = block * MAXT + 2 * pair
            list_ref[1, entry] = tiles_ref[block, 2 * pair]
            list_ref[2, entry] = jnp.where(2 * pair + 1 < live, tiles_ref[block, 2 * pair + 1], tile_total)
            return entry + 1

        return lax.fori_loop(0, (live + 1) // 2, one_pair, entry)

    entries = lax.fori_loop(0, blocks, one_block, 0)
    batches = (entries + BATCH - 1) // BATCH
    total_ref[0] = batches
    total_ref[1] = (entries + COUNTED - 1) // COUNTED

    def pad(entry, carry):
        list_ref[0, entry] = spare
        list_ref[1, entry] = tile_total
        list_ref[2, entry] = tile_total
        return carry

    lax.fori_loop(entries, batches * BATCH, pad, 0)

    commodity_rows = lax.broadcasted_iota(jnp.int32, (LB, PATHS_PER_BLOCK), 0)
    for block in range(blocks):
        group, j = block // GROUP, block % GROUP
        demand = demand_ref[:, group * LB : (group + 1) * LB].astype(F32).astype(BF16)
        onehot = (commodity_rows == comm_ref[block : block + 1, :] + COMMODITY_BLOCK * j).astype(F32).astype(BF16)
        same = lax.dot_general(onehot, onehot, (((0,), (0,)), ((), ())), preferred_element_type=F32)
        same_ref[block] = same.astype(BF16)
        wanted_ref[block] = jnp.dot(demand, onehot, preferred_element_type=F32) * DEMAND_UNIT


def build_listing(tile_total, block_tiles, block_count, path_commodity, demand):
    blocks = block_tiles.shape[0]
    given = stay(block_tiles, block_count, path_commodity, demand)
    return pl.pallas_call(
        lambda *refs: listing_kernel(tile_total, *refs),
        in_specs=[REMAIN] * 4,
        out_specs=[SCALARS, SCALARS, ARRAY, ARRAY],
        out_shape=[
            jax.ShapeDtypeStruct((LISTS, blocks * MAXT // 2 + BATCH), jnp.int32),
            jax.ShapeDtypeStruct((2,), jnp.int32),
            jax.ShapeDtypeStruct((blocks, PATHS_PER_BLOCK, PATHS_PER_BLOCK), BF16),
            jax.ShapeDtypeStruct((blocks, demand.shape[0], PATHS_PER_BLOCK), F32),
        ],
        scratch_shapes=[pltpu.SMEM(a.shape, a.dtype) for a in given[:2]]
        + [pltpu.VMEM(a.shape, a.dtype) for a in given[2:]]
        + [pltpu.SemaphoreType.DMA((4,))],
        compiler_params=pltpu.CompilerParams(vmem_limit_bytes=8 * MIB),
        cost_estimate=pl.CostEstimate(flops=10**9, bytes_accessed=10**7, transcendentals=0),
        name="listing",
    )(*given)


def incidence_kernel(list_ref, total_ref, given_ref, hits_ref, turned_ref, links_ref, arrived):
    copies = fetch([given_ref], [links_ref], arrived)
    blocks = links_ref.shape[1] // PATHS_PER_BLOCK
    for ref in (hits_ref, turned_ref):
        ref[-2 * LB :, :] = jnp.zeros((2 * LB, LB), BF16)
    lanes = [(lax.broadcasted_iota(jnp.int32, (PACK, LB), 0) + PACK * g).astype(F32).astype(BF16) for g in range(LB // PACK)]
    one, zero = jnp.ones((PACK, PATHS_PER_BLOCK), BF16), jnp.zeros((PACK, PATHS_PER_BLOCK), BF16)
    copies[0].wait()

    def count_step(step, carry):
        done = []
        for j in range(COUNTED):
            entry = step * COUNTED + j
            slot = list_ref[0, entry]
            block = jnp.minimum(slot // MAXT, blocks - 1)
            links = links_ref[:, aligned(block, PATHS_PER_BLOCK, PATHS_PER_BLOCK)]
            for side in range(2):
                place = (links - list_ref[1 + side, entry] * LB).astype(F32)
                counts = None
                for h in range(links.shape[0]):
                    row = jnp.broadcast_to(place[h : h + 1, :], (PACK, PATHS_PER_BLOCK)).astype(BF16)
                    hit = [jnp.where(row == lane, one, zero) for lane in lanes]
                    counts = hit if counts is None else [a + b for a, b in zip(counts, hit)]
                done.append((aligned(slot + side, LB, LB), jnp.concatenate(counts, axis=0)))
        for where, table in done:
            hits_ref[where, :] = table
            turned_ref[where, :] = table.T
        return carry

    lax.fori_loop(0, total_ref[1], count_step, 0)


def build_incidence(path_links, pairs, total):
    blocks = path_links.shape[1] // PATHS_PER_BLOCK
    slots = blocks * MAXT + 2
    return pl.pallas_call(
        incidence_kernel,
        in_specs=[SCALARS, SCALARS, REMAIN],
        out_specs=[ARRAY, ARRAY],
        out_shape=[
            jax.ShapeDtypeStruct((slots * LB, PATHS_PER_BLOCK), BF16),
            jax.ShapeDtypeStruct((slots * PATHS_PER_BLOCK, LB), BF16),
        ],
        scratch_shapes=[pltpu.VMEM(path_links.shape, path_links.dtype), pltpu.SemaphoreType.DMA((1,))],
        compiler_params=pltpu.CompilerParams(vmem_limit_bytes=8 * MIB),
        cost_estimate=pl.CostEstimate(flops=10**6, bytes_accessed=20 * 10**6, transcendentals=0),
        name="incidence",
    )(pairs, total, *stay(path_links))


def sweep(list_ref, total_ref, hits_ref, turned_ref, same_ref, wanted_at, put_flow, split_ref, cost_ref, flow_ref, load_ref):
    blocks, rows2 = same_ref.shape[0], cost_ref.shape[1]
    rows = rows2 // 2
    flow_ref[blocks] = jnp.zeros(flow_ref.shape[1:], BF16)
    split_ref[split_ref.shape[0] - 1] = jnp.zeros(split_ref.shape[1:], BF16)
    load_ref[...] = jnp.zeros_like(load_ref)
    cost_ref[...] = jnp.zeros_like(cost_ref)
    batches = total_ref[0]

    def cost_batch(batch, carry):
        done = []
        for j in range(BATCH):
            slot, left, right = (list_ref[i, batch * BATCH + j] for i in range(LISTS))
            block = slot // MAXT
            chosen = jnp.concatenate([split_ref[left], split_ref[right]], axis=1)
            done.append((block, jnp.dot(chosen, hits_ref[aligned(slot, 2 * LB, LB), :], preferred_element_type=F32)))
        for block, cost in done:
            cost_ref[block] += cost
        return carry

    lax.fori_loop(0, batches, cost_batch, 0)

    for block in range(blocks):
        weight = jnp.exp(-SOFTMIN_RATE * (cost_ref[block, :rows] + cost_ref[block, rows:]))
        total = jnp.dot(stacked(weight), same_ref[block], preferred_element_type=F32)
        flow = wanted_at(block) * weight / (total[:rows] + total[rows:])
        put_flow(block, flow)
        flow_ref[block] = stacked(flow)

    def load_batch(batch, carry):
        done = []
        for j in range(BATCH):
            slot, left, right = (list_ref[i, batch * BATCH + j] for i in range(LISTS))
            block = slot // MAXT
            for side, tile in enumerate((left, right)):
                turned = turned_ref[aligned(slot + side, LB, LB), :]
                done.append((tile, jnp.dot(flow_ref[block], turned, preferred_element_type=F32)))
        for tile, load in done:
            load_ref[tile] += load
        return carry

    lax.fori_loop(0, batches, load_batch, 0)


def spread(split_ref, first, shard):
    for k in range(shard.shape[-1] // LB):
        split_ref[first + k] = stacked(shard[:, k * LB : (k + 1) * LB])


def path_columns(block):
    return slice(block * PATHS_PER_BLOCK, (block + 1) * PATHS_PER_BLOCK)


def sweep_scratch(rows, tiles, blocks):
    return [
        pltpu.VMEM((tiles + 1, 2 * rows, LB), BF16),
        pltpu.VMEM((blocks + 1, 2 * rows, PATHS_PER_BLOCK), F32),
        pltpu.VMEM((blocks + 1, 2 * rows, PATHS_PER_BLOCK), BF16),
        pltpu.VMEM((tiles + 1, 2 * rows, LB), F32),
    ]


def sweep_cost(size):
    return pl.CostEstimate(flops=10**10, bytes_accessed=size, transcendentals=0)


def half_kernel(far, n, list_ref, total_ref, *refs):
    pieces, (hits_ref, turned_ref, same_ref, wanted_ref) = refs[:n], refs[n : n + 4]
    flows_ref, mine_ref, other_ref, *scratch = refs[-7:]
    z = lax.axis_index("path")
    rows = scratch[0].shape[1] // 2
    side = lax.div(z, 2)
    side = 1 - side if far else side
    shard_tiles = pieces[0].shape[1] // LB
    for m, piece in enumerate(pieces):
        start = side if piece.shape[0] == 2 * rows else 0
        spread(scratch[0], (z ^ m) * shard_tiles, piece[aligned(start, rows, rows), :])

    def wanted_at(block):
        return wanted_ref[block, aligned(side, rows, rows), :]

    def put_flow(block, flow):
        flows_ref[:, path_columns(block)] = flow

    sweep(list_ref, total_ref, hits_ref, turned_ref, same_ref, wanted_at, put_flow, *scratch)
    load_ref = scratch[3]
    height = rows // 2
    for out_ref, place in ((mine_ref, lax.rem(z, 2)), (other_ref, 1 - lax.rem(z, 2))):
        for k in range(load_ref.shape[0] - 1):
            high = load_ref[k, aligned(place, height, height), :]
            out_ref[k] = high + load_ref[k, pl.ds(pl.multiple_of(rows + place * height, height), height), :]


def half_sweep(pieces, rows, built, far):
    hits, turned, pairs, total, same, wanted = built
    own = pieces[0].shape[1]
    n = len(pieces)
    blocks = wanted.shape[0]
    tiles = n * own // LB
    return pl.pallas_call(
        lambda *refs: half_kernel(far, n, *refs),
        in_specs=[SCALARS, SCALARS] + [ARRAY] * (n + 4),
        out_specs=[ARRAY] * 3,
        out_shape=[jax.ShapeDtypeStruct((rows, blocks * PATHS_PER_BLOCK), F32)]
        + [jax.ShapeDtypeStruct((tiles, rows // 2, LB), F32)] * 2,
        scratch_shapes=sweep_scratch(rows, tiles, blocks),
        compiler_params=pltpu.CompilerParams(vmem_limit_bytes=16 * MIB),
        cost_estimate=sweep_cost(25 * 10**6),
        name="far_sweep" if far else "near_sweep",
    )(pairs, total, *pieces, hits, turned, same, wanted)


def wide_kernel(list_ref, total_ref, lengths_ref, hits_ref, turned_ref, same_ref, wanted_ref, flows_ref, out_ref, *scratch):
    shards, _, own = lengths_ref.shape
    rows = lengths_ref.shape[1]

    def one_shard(i, carry):
        spread(scratch[0], i * (own // LB), lengths_ref[i])
        return carry

    lax.fori_loop(0, shards, one_shard, 0)

    def put_flow(block, flow):
        flows_ref[:, path_columns(block)] = flow

    sweep(
        list_ref, total_ref, hits_ref, turned_ref, same_ref, lambda block: wanted_ref[block], put_flow, *scratch
    )
    out_ref[...] = scratch[3][:-1, :rows, :] + scratch[3][:-1, rows:, :]


def wide_sweep(lengths, built):
    hits, turned, pairs, total, same, wanted = built
    shards, rows, own = lengths.shape
    blocks = wanted.shape[0]
    tiles = shards * own // LB
    return pl.pallas_call(
        wide_kernel,
        in_specs=[SCALARS, SCALARS] + [ARRAY] * 5,
        out_specs=[ARRAY] * 2,
        out_shape=[
            jax.ShapeDtypeStruct((rows, blocks * PATHS_PER_BLOCK), F32),
            jax.ShapeDtypeStruct((tiles, rows, LB), F32),
        ],
        scratch_shapes=sweep_scratch(rows, tiles, blocks),
        compiler_params=pltpu.CompilerParams(vmem_limit_bytes=48 * MIB),
        cost_estimate=sweep_cost(10**7),
        name="wide_sweep",
    )(pairs, total, lengths, hits, turned, same, wanted)


def growth_kernel(n, parts, *refs):
    lengths, capacities, weight_ref = refs[:n], refs[n : 2 * n], refs[2 * n]
    loads = refs[2 * n + 1 : 2 * n + 1 + parts]
    next_refs, mixed_ref, grown_ref = refs[-n - 2 : -2], refs[-2], refs[-1]
    z = lax.axis_index("path")
    links_total, height, _ = grown_ref.shape
    shard_tiles = links_total // n
    total = jnp.zeros((height, LB), F32)
    for m in range(n):
        row = aligned(z if lengths[m].shape[0] == n * height else lax.rem(z, 2), height, height)
        first = (z ^ m) * shard_tiles
        for k in range(shard_tiles):
            columns = slice(k * LB, (k + 1) * LB)
            load = loads[0][first + k]
            for ref in loads[1:]:
                load = load + ref[first + k]
            grown = lengths[m][row, columns] * jnp.exp(STEP_RATE * load / capacities[m][:, columns])
            grown_ref[m * shard_tiles + k] = grown
            total = total + grown
    factor = (links_total * LB) / jnp.sum(total, axis=1, keepdims=True)
    weight = weight_ref[aligned(z, height, height), :]
    for m in range(n):
        first = (z ^ m) * shard_tiles
        for k in range(shard_tiles):
            new = grown_ref[m * shard_tiles + k] * factor
            next_refs[m][:, k * LB : (k + 1) * LB] = new
            mixed_ref[pl.ds(first + k, 1), :] = jnp.sum(weight * new, axis=0, keepdims=True)


def grow(loads, lengths, capacities, weights):
    n, parts = len(lengths), len(loads)
    tiles, height, _ = loads[0].shape
    return pl.pallas_call(
        lambda *refs: growth_kernel(n, parts, *refs),
        in_specs=[ARRAY] * (2 * n + 1 + parts),
        out_specs=[ARRAY] * (n + 1),
        out_shape=[jax.ShapeDtypeStruct((height, tiles * LB // n), F32)] * n + [jax.ShapeDtypeStruct((tiles, LB), F32)],
        scratch_shapes=[pltpu.VMEM((tiles, height, LB), F32)],
        compiler_params=pltpu.CompilerParams(vmem_limit_bytes=8 * MIB),
        cost_estimate=pl.CostEstimate(flops=10**6, bytes_accessed=5 * 10**6, transcendentals=10**5),
        name="growth",
    )(*lengths, *capacities, weights, *loads)


def robust_kernel(parts, links_ref, *refs):
    part_refs, (out_ref, mixed_ref) = refs[:parts], refs[parts:]
    blocks = out_ref.shape[0]
    hops = links_ref.shape[0]
    mixed = part_refs[0][...]
    for ref in part_refs[1:]:
        mixed = mixed + ref[...]
    mixed_ref[...] = mixed
    for first in range(0, blocks, TOGETHER):
        group = range(first, min(first + TOGETHER, blocks))
        links = [links_ref[:, path_columns(block)] for block in group]

        def one_tile(tile, costs):
            table = jnp.broadcast_to(mixed_ref[pl.ds(tile, 1), :], (hops, LB))
            found = [jnp.take_along_axis(table, x & (LB - 1), axis=1) for x in links]
            return [jnp.where((x >> LB_BITS) == tile, f, c) for x, f, c in zip(links, found, costs)]

        tiles = mixed_ref.shape[0]
        costs = [jnp.zeros((hops, PATHS_PER_BLOCK), F32)] * len(links)
        step = UNROLL if tiles % UNROLL == 0 else 1

        def some_tiles(i, costs):
            for j in range(step):
                costs = one_tile(i * step + j, costs)
            return costs

        costs = lax.fori_loop(0, tiles // step, some_tiles, costs)
        for block, cost in zip(group, costs):
            out_ref[block : block + 1, :] = jnp.sum(cost, axis=0, keepdims=True) / S


def robust_costs(path_links, parts):
    hops, paths = path_links.shape
    blocks = paths // PATHS_PER_BLOCK
    out = pl.pallas_call(
        lambda *refs: robust_kernel(len(parts), *refs),
        in_specs=[ARRAY] * (len(parts) + 1),
        out_specs=ARRAY,
        out_shape=jax.ShapeDtypeStruct((blocks, PATHS_PER_BLOCK), F32),
        scratch_shapes=[pltpu.VMEM(parts[0].shape, F32)],
        compiler_params=pltpu.CompilerParams(vmem_limit_bytes=8 * MIB),
        cost_estimate=pl.CostEstimate(flops=10**6, bytes_accessed=10**6, transcendentals=0),
        name="robust",
    )(path_links, *parts)
    return out.reshape(-1)


def exchange(x, axis, n, bit):
    return lax.ppermute(x, axis, [(i, i ^ bit) for i in range(n)])


def body_paired(sizes, path_links, block_tiles, block_count, path_commodity, demand, lengths, capacity, scenario_weight):
    n = sizes["path"]
    rows, own = lengths.shape
    half, height = rows // 2, rows // n
    z = lax.axis_index("path").astype(jnp.int32)
    side = z // 2
    far = lax.dynamic_slice(lengths, ((1 - side) * half, 0), (half, own))
    near = lax.dynamic_slice(lengths, (side * half, 0), (half, own))

    def swap(x, m):
        return exchange(x, "path", n, m)

    shared = swap(lengths, 1)
    far_pieces = [far, shared, swap(near, 2), swap(near, 3)]
    pairs, total, same, wanted = build_listing(n * own // LB, block_tiles, block_count, path_commodity, demand)
    late, same = lax.optimization_barrier((far, same))
    near_pieces = [near, shared, swap(late, 2), swap(late, 3)]
    built = (*build_incidence(path_links, pairs, total), pairs, total, same, wanted)
    far_flows, straight, crossed = half_sweep(far_pieces, half, built, True)
    partial = straight + swap(crossed, 1)
    near_flows, mine, other = half_sweep(near_pieces, half, built, False)
    partial, other = lax.optimization_barrier((partial, other))
    loads = [mine, swap(other, 1), swap(partial, 2)]
    capacity_row = capacity[None, :]
    capacities = [capacity_row] + [swap(capacity_row, m) for m in range(1, n)]
    *new, mixed = grow(loads, near_pieces, capacities, scenario_weight[:, None])
    mixed = mixed + exchange(mixed, "sub", 2, 1)
    mixed = mixed + exchange(mixed, "scen", 2, 1)
    mixed = mixed + swap(mixed, 1)
    parts = [mixed, swap(mixed, 2)]
    arrived = [new[0]] + [swap(new[m], m) for m in range(1, n)]
    robust = robust_costs(path_links, parts)
    lengths_next = jnp.zeros((rows, own), F32)
    for m in range(n):
        lengths_next = lax.dynamic_update_slice(lengths_next, arrived[m], ((z ^ m) * height, 0))
    first, second = jnp.where(side == 0, near_flows, far_flows), jnp.where(side == 0, far_flows, near_flows)
    return jnp.concatenate([first, second], axis=0), lengths_next, robust


def body_wide(sizes, path_links, block_tiles, block_count, path_commodity, demand, lengths, capacity, scenario_weight):
    gathered = lax.all_gather(lengths, "path", axis=0, tiled=False)
    pairs, total, same, wanted = build_listing(gathered.shape[0] * gathered.shape[2] // LB, block_tiles, block_count, path_commodity, demand)
    built = (*build_incidence(path_links, pairs, total), pairs, total, same, wanted)
    flows, loads = wide_sweep(gathered, built)
    loads = loads.transpose(1, 0, 2).reshape(lengths.shape[0], -1)
    own_loads = lax.psum_scatter(loads, "path", scatter_dimension=1, tiled=True)
    grown = lengths * jnp.exp(STEP_RATE * own_loads / capacity[None, :])
    totals = lax.psum(jnp.sum(grown, axis=1), "path")
    lengths_next = grown * (loads.shape[1] / totals)[:, None]
    mixed = lax.psum(jnp.sum(lengths_next * scenario_weight[:, None], axis=0), ("scen", "sub"))
    mixed = lax.all_gather(mixed.reshape(-1, LB), "path", axis=0, tiled=True)
    return flows, lengths_next, robust_costs(path_links, [mixed])


def solution(mesh):
    sizes = dict(mesh.shape)

    def body(*args):
        paired = sizes["path"] == 4 and sizes["scen"] == 2 and sizes["sub"] == 2 and args[5].shape[0] % 64 == 0
        return (body_paired if paired else body_wide)(sizes, *args)

    return jax.shard_map(
        body,
        mesh=mesh,
        in_specs=(
            P(None, ("grp", "path")),
            P(("grp", "path"), None),
            P(("grp", "path")),
            P(("grp", "path"), None),
            P(("scen", "sub"), ("grp", "path")),
            P(("scen", "sub"), ("grp", "path")),
            P(("grp", "path")),
            P(("grp", "scen", "sub")),
        ),
        out_specs=(
            P(("scen", "sub"), ("grp", "path")),
            P(("scen", "sub"), ("grp", "path")),
            P(("grp", "path")),
        ),
        check_vma=False,
    )
```

```python
import jax
import jax.numpy as jnp
from jax import lax
from jax.experimental import pallas as pl
from jax.experimental.pallas import tpu as pltpu
from jax.sharding import PartitionSpec as P

PATHS_PER_BLOCK = 128
LB = 128
MAXT = 16
COMMODITY_BLOCK = 32
S = 256

SOFTMIN_RATE = 0.25
STEP_RATE = 1.0
DEMAND_UNIT = 0.0625
MIB = 1024 * 1024

F32 = jnp.float32
BF16 = jnp.bfloat16
PACK = 16
BATCH = 16
GROUP = LB // COMMODITY_BLOCK

SCALARS = pl.BlockSpec(memory_space=pltpu.SMEM)
ARRAY = pl.BlockSpec(memory_space=pltpu.VMEM)
LISTS = 3
TOGETHER = 8
UNROLL = 28
LB_BITS = 7
COUNTED = 8


def split(x):
    high = x.astype(BF16)
    return high, (x - high.astype(F32)).astype(BF16)


def stacked(x):
    return jnp.concatenate(split(x), axis=0)


def aligned(start, size, unit):
    return pl.ds(pl.multiple_of(start * unit, unit), size)


def stay(*arrays):
    return tuple(pltpu.with_memory_space_constraint(a, pltpu.HBM) for a in arrays)


REMAIN = pl.BlockSpec(memory_space=pltpu.HBM)


def fetch(given, local, arrived):
    copies = [pltpu.make_async_copy(a, b, arrived.at[i]) for i, (a, b) in enumerate(zip(given, local))]
    for copy in copies:
        copy.start()
    return copies


def listing_kernel(tile_total, *refs):
    given, (list_ref, total_ref, same_ref, wanted_ref, kept_ref) = refs[:5], refs[5:10]
    local, arrived = refs[10:15], refs[15]
    tiles_ref, count_ref, comm_ref, demand_ref, capacity_ref = local
    copies = fetch(given, local, arrived)
    blocks = tiles_ref.shape[0]
    spare = blocks * MAXT
    for copy in copies:
        copy.wait()

    def one_block(block, entry):
        live = count_ref[block]

        def one_pair(pair, entry):
            list_ref[0, entry] = block * MAXT + 2 * pair
            list_ref[1, entry] = tiles_ref[block, 2 * pair]
            list_ref[2, entry] = jnp.where(2 * pair + 1 < live, tiles_ref[block, 2 * pair + 1], tile_total)
            return entry + 1

        return lax.fori_loop(0, (live + 1) // 2, one_pair, entry)

    entries = lax.fori_loop(0, blocks, one_block, 0)
    batches = (entries + BATCH - 1) // BATCH
    total_ref[0] = batches
    total_ref[1] = (entries + COUNTED - 1) // COUNTED

    def pad(entry, carry):
        list_ref[0, entry] = spare
        list_ref[1, entry] = tile_total
        list_ref[2, entry] = tile_total
        return carry

    lax.fori_loop(entries, batches * BATCH, pad, 0)
    kept_ref[...] = capacity_ref[...]

    commodity_rows = lax.broadcasted_iota(jnp.int32, (LB, PATHS_PER_BLOCK), 0)
    for block in range(blocks):
        group, j = block // GROUP, block % GROUP
        demand = demand_ref[:, group * LB : (group + 1) * LB].astype(F32).astype(BF16)
        onehot = (commodity_rows == comm_ref[block : block + 1, :] + COMMODITY_BLOCK * j).astype(F32).astype(BF16)
        same = lax.dot_general(onehot, onehot, (((0,), (0,)), ((), ())), preferred_element_type=F32)
        same_ref[block] = same.astype(BF16)
        wanted_ref[block] = jnp.dot(demand, onehot, preferred_element_type=F32) * DEMAND_UNIT


def build_listing(tile_total, block_tiles, block_count, path_commodity, demand, capacity):
    blocks = block_tiles.shape[0]
    given = stay(block_tiles, block_count, path_commodity, demand, capacity.reshape(-1, LB))
    return pl.pallas_call(
        lambda *refs: listing_kernel(tile_total, *refs),
        in_specs=[REMAIN] * 5,
        out_specs=[SCALARS, SCALARS, ARRAY, ARRAY, ARRAY],
        out_shape=[
            jax.ShapeDtypeStruct((LISTS, blocks * MAXT // 2 + BATCH), jnp.int32),
            jax.ShapeDtypeStruct((2,), jnp.int32),
            jax.ShapeDtypeStruct((blocks, PATHS_PER_BLOCK, PATHS_PER_BLOCK), BF16),
            jax.ShapeDtypeStruct((blocks, demand.shape[0], PATHS_PER_BLOCK), F32),
            jax.ShapeDtypeStruct(given[4].shape, F32),
        ],
        scratch_shapes=[pltpu.SMEM(a.shape, a.dtype) for a in given[:2]]
        + [pltpu.VMEM(a.shape, a.dtype) for a in given[2:]]
        + [pltpu.SemaphoreType.DMA((5,))],
        compiler_params=pltpu.CompilerParams(vmem_limit_bytes=8 * MIB),
        cost_estimate=pl.CostEstimate(flops=10**9, bytes_accessed=10**7, transcendentals=0),
        name="listing",
    )(*given)


def incidence_kernel(list_ref, total_ref, given_ref, hits_ref, turned_ref, links_ref, arrived):
    copies = fetch([given_ref], [links_ref], arrived)
    blocks = links_ref.shape[1] // PATHS_PER_BLOCK
    for ref in (hits_ref, turned_ref):
        ref[-2 * LB :, :] = jnp.zeros((2 * LB, LB), BF16)
    lanes = [(lax.broadcasted_iota(jnp.int32, (PACK, LB), 0) + PACK * g).astype(F32).astype(BF16) for g in range(LB // PACK)]
    one, zero = jnp.ones((PACK, PATHS_PER_BLOCK), BF16), jnp.zeros((PACK, PATHS_PER_BLOCK), BF16)
    copies[0].wait()

    def count_step(step, carry):
        done = []
        for j in range(COUNTED):
            entry = step * COUNTED + j
            slot = list_ref[0, entry]
            block = jnp.minimum(slot // MAXT, blocks - 1)
            links = links_ref[:, aligned(block, PATHS_PER_BLOCK, PATHS_PER_BLOCK)]
            for side in range(2):
                place = (links - list_ref[1 + side, entry] * LB).astype(F32)
                counts = None
                for h in range(links.shape[0]):
                    row = jnp.broadcast_to(place[h : h + 1, :], (PACK, PATHS_PER_BLOCK)).astype(BF16)
                    hit = [jnp.where(row == lane, one, zero) for lane in lanes]
                    counts = hit if counts is None else [a + b for a, b in zip(counts, hit)]
                done.append((aligned(slot + side, LB, LB), jnp.concatenate(counts, axis=0)))
        for where, table in done:
            hits_ref[where, :] = table
            turned_ref[where, :] = table.T
        return carry

    lax.fori_loop(0, total_ref[1], count_step, 0)


def build_incidence(path_links, pairs, total):
    blocks = path_links.shape[1] // PATHS_PER_BLOCK
    slots = blocks * MAXT + 2
    return pl.pallas_call(
        incidence_kernel,
        in_specs=[SCALARS, SCALARS, REMAIN],
        out_specs=[ARRAY, ARRAY],
        out_shape=[
            jax.ShapeDtypeStruct((slots * LB, PATHS_PER_BLOCK), BF16),
            jax.ShapeDtypeStruct((slots * PATHS_PER_BLOCK, LB), BF16),
        ],
        scratch_shapes=[pltpu.VMEM(path_links.shape, path_links.dtype), pltpu.SemaphoreType.DMA((1,))],
        compiler_params=pltpu.CompilerParams(vmem_limit_bytes=8 * MIB),
        cost_estimate=pl.CostEstimate(flops=10**6, bytes_accessed=20 * 10**6, transcendentals=0),
        name="incidence",
    )(pairs, total, *stay(path_links))


def sweep(list_ref, total_ref, hits_ref, turned_ref, same_ref, wanted_at, put_flow, split_ref, cost_ref, flow_ref, load_ref):
    blocks, rows2 = same_ref.shape[0], cost_ref.shape[1]
    rows = rows2 // 2
    flow_ref[blocks] = jnp.zeros(flow_ref.shape[1:], BF16)
    split_ref[split_ref.shape[0] - 1] = jnp.zeros(split_ref.shape[1:], BF16)
    load_ref[...] = jnp.zeros_like(load_ref)
    cost_ref[...] = jnp.zeros_like(cost_ref)
    batches = total_ref[0]

    def cost_batch(batch, carry):
        done = []
        for j in range(BATCH):
            slot, left, right = (list_ref[i, batch * BATCH + j] for i in range(LISTS))
            block = slot // MAXT
            chosen = jnp.concatenate([split_ref[left], split_ref[right]], axis=1)
            done.append((block, jnp.dot(chosen, hits_ref[aligned(slot, 2 * LB, LB), :], preferred_element_type=F32)))
        for block, cost in done:
            cost_ref[block] += cost
        return carry

    lax.fori_loop(0, batches, cost_batch, 0)

    for block in range(blocks):
        weight = jnp.exp(-SOFTMIN_RATE * (cost_ref[block, :rows] + cost_ref[block, rows:]))
        total = jnp.dot(stacked(weight), same_ref[block], preferred_element_type=F32)
        flow = wanted_at(block) * weight / (total[:rows] + total[rows:])
        put_flow(block, flow)
        flow_ref[block] = stacked(flow)

    def load_batch(batch, carry):
        done = []
        for j in range(BATCH):
            slot, left, right = (list_ref[i, batch * BATCH + j] for i in range(LISTS))
            block = slot // MAXT
            for side, tile in enumerate((left, right)):
                turned = turned_ref[aligned(slot + side, LB, LB), :]
                done.append((tile, jnp.dot(flow_ref[block], turned, preferred_element_type=F32)))
        for tile, load in done:
            load_ref[tile] += load
        return carry

    lax.fori_loop(0, batches, load_batch, 0)


def spread(split_ref, first, shard):
    for k in range(shard.shape[-1] // LB):
        split_ref[first + k] = stacked(shard[:, k * LB : (k + 1) * LB])


def path_columns(block):
    return slice(block * PATHS_PER_BLOCK, (block + 1) * PATHS_PER_BLOCK)


def sweep_scratch(rows, tiles, blocks):
    return [
        pltpu.VMEM((tiles + 1, 2 * rows, LB), BF16),
        pltpu.VMEM((blocks + 1, 2 * rows, PATHS_PER_BLOCK), F32),
        pltpu.VMEM((blocks + 1, 2 * rows, PATHS_PER_BLOCK), BF16),
        pltpu.VMEM((tiles + 1, 2 * rows, LB), F32),
    ]


def sweep_cost(size):
    return pl.CostEstimate(flops=10**10, bytes_accessed=size, transcendentals=0)


def half_kernel(far, n, list_ref, total_ref, *refs):
    pieces, (hits_ref, turned_ref, same_ref, wanted_ref, capacity_ref) = refs[:n], refs[n : n + 5]
    flows_ref, mine_ref, other_ref, *scratch = refs[-7:]
    z = lax.axis_index("path")
    rows = scratch[0].shape[1] // 2
    side = lax.div(z, 2)
    side = 1 - side if far else side
    shard_tiles = pieces[0].shape[1] // LB
    for m, piece in enumerate(pieces):
        start = side if piece.shape[0] == 2 * rows else 0
        spread(scratch[0], (z ^ m) * shard_tiles, piece[aligned(start, rows, rows), :])

    def wanted_at(block):
        return wanted_ref[block, aligned(side, rows, rows), :]

    def put_flow(block, flow):
        flows_ref[:, path_columns(block)] = flow

    sweep(list_ref, total_ref, hits_ref, turned_ref, same_ref, wanted_at, put_flow, *scratch)
    load_ref = scratch[3]
    height = rows // 2
    for out_ref, place in ((mine_ref, lax.rem(z, 2)), (other_ref, 1 - lax.rem(z, 2))):
        for k in range(load_ref.shape[0] - 1):
            high = load_ref[k, aligned(place, height, height), :]
            out_ref[k] = high + load_ref[k, pl.ds(pl.multiple_of(rows + place * height, height), height), :]
    for out_ref, start in ((mine_ref, 0), (other_ref, height // 2 if far else 0)):
        out_ref[load_ref.shape[0] - 1] = jnp.zeros((height, LB), F32)
        out_ref[load_ref.shape[0] - 1, start : start + shard_tiles, :] = capacity_ref[...]


def half_sweep(pieces, rows, built, capacity, far):
    hits, turned, pairs, total, same, wanted = built
    own = pieces[0].shape[1]
    n = len(pieces)
    blocks = wanted.shape[0]
    tiles = n * own // LB
    return pl.pallas_call(
        lambda *refs: half_kernel(far, n, *refs),
        in_specs=[SCALARS, SCALARS] + [ARRAY] * (n + 5),
        out_specs=[ARRAY] * 3,
        out_shape=[jax.ShapeDtypeStruct((rows, blocks * PATHS_PER_BLOCK), F32)]
        + [jax.ShapeDtypeStruct((tiles + 1, rows // 2, LB), F32)] * 2,
        scratch_shapes=sweep_scratch(rows, tiles, blocks),
        compiler_params=pltpu.CompilerParams(vmem_limit_bytes=16 * MIB),
        cost_estimate=sweep_cost(25 * 10**6),
        name="far_sweep" if far else "near_sweep",
    )(pairs, total, *pieces, hits, turned, same, wanted, capacity)


def wide_kernel(list_ref, total_ref, lengths_ref, hits_ref, turned_ref, same_ref, wanted_ref, flows_ref, out_ref, *scratch):
    shards, _, own = lengths_ref.shape
    rows = lengths_ref.shape[1]

    def one_shard(i, carry):
        spread(scratch[0], i * (own // LB), lengths_ref[i])
        return carry

    lax.fori_loop(0, shards, one_shard, 0)

    def put_flow(block, flow):
        flows_ref[:, path_columns(block)] = flow

    sweep(
        list_ref, total_ref, hits_ref, turned_ref, same_ref, lambda block: wanted_ref[block], put_flow, *scratch
    )
    out_ref[...] = scratch[3][:-1, :rows, :] + scratch[3][:-1, rows:, :]


def wide_sweep(lengths, built):
    hits, turned, pairs, total, same, wanted = built
    shards, rows, own = lengths.shape
    blocks = wanted.shape[0]
    tiles = shards * own // LB
    return pl.pallas_call(
        wide_kernel,
        in_specs=[SCALARS, SCALARS] + [ARRAY] * 5,
        out_specs=[ARRAY] * 2,
        out_shape=[
            jax.ShapeDtypeStruct((rows, blocks * PATHS_PER_BLOCK), F32),
            jax.ShapeDtypeStruct((tiles, rows, LB), F32),
        ],
        scratch_shapes=sweep_scratch(rows, tiles, blocks),
        compiler_params=pltpu.CompilerParams(vmem_limit_bytes=48 * MIB),
        cost_estimate=sweep_cost(10**7),
        name="wide_sweep",
    )(pairs, total, lengths, hits, turned, same, wanted)


def growth_kernel(n, parts, *refs):
    lengths, (capacity_ref, weight_ref) = refs[:n], refs[n : n + 2]
    loads = refs[n + 2 : n + 2 + parts]
    next_refs, mixed_ref, grown_ref = refs[-n - 2 : -2], refs[-2], refs[-1]
    z = lax.axis_index("path")
    links_total, height, _ = grown_ref.shape
    shard_tiles = links_total // n
    total = jnp.zeros((height, LB), F32)
    own, near, far = capacity_ref[...], loads[1][links_total], loads[2][links_total]
    capacities = (own, near, far, far[height // 2 :])
    for m in range(n):
        row = aligned(z if lengths[m].shape[0] == n * height else lax.rem(z, 2), height, height)
        first = (z ^ m) * shard_tiles
        for k in range(shard_tiles):
            columns = slice(k * LB, (k + 1) * LB)
            load = loads[0][first + k]
            for ref in loads[1:]:
                load = load + ref[first + k]
            grown = lengths[m][row, columns] * jnp.exp(STEP_RATE * load / capacities[m][k : k + 1])
            grown_ref[m * shard_tiles + k] = grown
            total = total + grown
    factor = (links_total * LB) / jnp.sum(total, axis=1, keepdims=True)
    weight = weight_ref[aligned(z, height, height), :]
    for m in range(n):
        first = (z ^ m) * shard_tiles
        for k in range(shard_tiles):
            new = grown_ref[m * shard_tiles + k] * factor
            next_refs[m][:, k * LB : (k + 1) * LB] = new
            mixed_ref[pl.ds(first + k, 1), :] = jnp.sum(weight * new, axis=0, keepdims=True)


def grow(loads, lengths, capacity, weights):
    n, parts = len(lengths), len(loads)
    tiles, height = loads[0].shape[0] - 1, loads[0].shape[1]
    return pl.pallas_call(
        lambda *refs: growth_kernel(n, parts, *refs),
        in_specs=[ARRAY] * (n + 2 + parts),
        out_specs=[ARRAY] * (n + 1),
        out_shape=[jax.ShapeDtypeStruct((height, tiles * LB // n), F32)] * n + [jax.ShapeDtypeStruct((tiles, LB), F32)],
        scratch_shapes=[pltpu.VMEM((tiles, height, LB), F32)],
        compiler_params=pltpu.CompilerParams(vmem_limit_bytes=8 * MIB),
        cost_estimate=pl.CostEstimate(flops=10**6, bytes_accessed=5 * 10**6, transcendentals=10**5),
        name="growth",
    )(*lengths, capacity, weights, *loads)


def robust_kernel(parts, links_ref, *refs):
    part_refs, (out_ref, mixed_ref) = refs[:parts], refs[parts:]
    blocks = out_ref.shape[0]
    hops = links_ref.shape[0]
    mixed = part_refs[0][...]
    for ref in part_refs[1:]:
        mixed = mixed + ref[...]
    mixed_ref[...] = mixed
    for first in range(0, blocks, TOGETHER):
        group = range(first, min(first + TOGETHER, blocks))
        links = [links_ref[:, path_columns(block)] for block in group]

        def one_tile(tile, costs):
            table = jnp.broadcast_to(mixed_ref[pl.ds(tile, 1), :], (hops, LB))
            found = [jnp.take_along_axis(table, x & (LB - 1), axis=1) for x in links]
            return [jnp.where((x >> LB_BITS) == tile, f, c) for x, f, c in zip(links, found, costs)]

        tiles = mixed_ref.shape[0]
        costs = [jnp.zeros((hops, PATHS_PER_BLOCK), F32)] * len(links)
        step = UNROLL if tiles % UNROLL == 0 else 1

        def some_tiles(i, costs):
            for j in range(step):
                costs = one_tile(i * step + j, costs)
            return costs

        costs = lax.fori_loop(0, tiles // step, some_tiles, costs)
        for block, cost in zip(group, costs):
            out_ref[block : block + 1, :] = jnp.sum(cost, axis=0, keepdims=True) / S


def robust_costs(path_links, parts):
    hops, paths = path_links.shape
    blocks = paths // PATHS_PER_BLOCK
    out = pl.pallas_call(
        lambda *refs: robust_kernel(len(parts), *refs),
        in_specs=[ARRAY] * (len(parts) + 1),
        out_specs=ARRAY,
        out_shape=jax.ShapeDtypeStruct((blocks, PATHS_PER_BLOCK), F32),
        scratch_shapes=[pltpu.VMEM(parts[0].shape, F32)],
        compiler_params=pltpu.CompilerParams(vmem_limit_bytes=8 * MIB),
        cost_estimate=pl.CostEstimate(flops=10**6, bytes_accessed=10**6, transcendentals=0),
        name="robust",
    )(path_links, *parts)
    return out.reshape(-1)


def exchange(x, axis, n, bit):
    return lax.ppermute(x, axis, [(i, i ^ bit) for i in range(n)])


def body_paired(sizes, path_links, block_tiles, block_count, path_commodity, demand, lengths, capacity, scenario_weight):
    n = sizes["path"]
    rows, own = lengths.shape
    half, height = rows // 2, rows // n
    z = lax.axis_index("path").astype(jnp.int32)
    side = z // 2
    far = lax.dynamic_slice(lengths, ((1 - side) * half, 0), (half, own))
    near = lax.dynamic_slice(lengths, (side * half, 0), (half, own))

    def swap(x, m):
        return exchange(x, "path", n, m)

    shared = swap(lengths, 1)
    far_pieces = [far, shared, swap(near, 2), swap(near, 3)]
    pairs, total, same, wanted, capacity_tiles = build_listing(
        n * own // LB, block_tiles, block_count, path_commodity, demand, capacity
    )
    straight_rows = swap(far, 2)
    near_pieces = [near, shared, straight_rows, swap(straight_rows, 1)]
    built = (*build_incidence(path_links, pairs, total), pairs, total, same, wanted)
    far_flows, straight, crossed = half_sweep(far_pieces, half, built, capacity_tiles, True)
    partial = straight + swap(crossed, 1)
    near_flows, mine, other = half_sweep(near_pieces, half, built, capacity_tiles, False)
    partial, other, near_flows = lax.optimization_barrier((partial, other, near_flows))
    loads = [mine, swap(other, 1), swap(partial, 2)]
    first, second = jnp.where(side == 0, near_flows, far_flows), jnp.where(side == 0, far_flows, near_flows)
    flows = jnp.concatenate([first, second], axis=0)
    weight_column = scenario_weight[:, None]
    flows, weight_column = lax.optimization_barrier((flows, weight_column))
    *new, mixed = grow(loads, near_pieces, capacity_tiles, weight_column)
    mixed = mixed + exchange(mixed, "sub", 2, 1)
    mixed = mixed + exchange(mixed, "scen", 2, 1)
    mixed = mixed + swap(mixed, 1)
    parts = [mixed, swap(mixed, 2)]
    arrived = [new[0]] + [swap(new[m], m) for m in range(1, n)]
    lengths_next = jnp.zeros((rows, own), F32)
    for m in range(n):
        lengths_next = lax.dynamic_update_slice(lengths_next, arrived[m], ((z ^ m) * height, 0))
    parts[1], lengths_next = lax.optimization_barrier((parts[1], lengths_next))
    robust = robust_costs(path_links, parts)
    return flows, lengths_next, robust


def body_wide(sizes, path_links, block_tiles, block_count, path_commodity, demand, lengths, capacity, scenario_weight):
    gathered = lax.all_gather(lengths, "path", axis=0, tiled=False)
    tiles = gathered.shape[0] * gathered.shape[2] // LB
    pairs, total, same, wanted, _ = build_listing(tiles, block_tiles, block_count, path_commodity, demand, capacity)
    built = (*build_incidence(path_links, pairs, total), pairs, total, same, wanted)
    flows, loads = wide_sweep(gathered, built)
    loads = loads.transpose(1, 0, 2).reshape(lengths.shape[0], -1)
    own_loads = lax.psum_scatter(loads, "path", scatter_dimension=1, tiled=True)
    grown = lengths * jnp.exp(STEP_RATE * own_loads / capacity[None, :])
    totals = lax.psum(jnp.sum(grown, axis=1), "path")
    lengths_next = grown * (loads.shape[1] / totals)[:, None]
    mixed = lax.psum(jnp.sum(lengths_next * scenario_weight[:, None], axis=0), ("scen", "sub"))
    mixed = lax.all_gather(mixed.reshape(-1, LB), "path", axis=0, tiled=True)
    return flows, lengths_next, robust_costs(path_links, [mixed])


def solution(mesh):
    sizes = dict(mesh.shape)

    def body(*args):
        paired = sizes["path"] == 4 and sizes["scen"] == 2 and sizes["sub"] == 2 and args[5].shape[0] % 64 == 0 and args[5].shape[1] // LB <= args[5].shape[0] // 8
        return (body_paired if paired else body_wide)(sizes, *args)

    return jax.shard_map(
        body,
        mesh=mesh,
        in_specs=(
            P(None, ("grp", "path")),
            P(("grp", "path"), None),
            P(("grp", "path")),
            P(("grp", "path"), None),
            P(("scen", "sub"), ("grp", "path")),
            P(("scen", "sub"), ("grp", "path")),
            P(("grp", "path")),
            P(("grp", "scen", "sub")),
        ),
        out_specs=(
            P(("scen", "sub"), ("grp", "path")),
            P(("scen", "sub"), ("grp", "path")),
            P(("grp", "path")),
        ),
        check_vma=False,
    )
```

```python
import jax
import jax.numpy as jnp
from jax import lax
from jax.experimental import pallas as pl
from jax.experimental.pallas import tpu as pltpu
from jax.sharding import PartitionSpec as P

PATHS_PER_BLOCK = 128
LB = 128
MAXT = 16
COMMODITY_BLOCK = 32
S = 256

SOFTMIN_RATE = 0.25
STEP_RATE = 1.0
DEMAND_UNIT = 0.0625
MIB = 1024 * 1024

F32 = jnp.float32
BF16 = jnp.bfloat16
PACK = 16
BATCH = 16
GROUP = LB // COMMODITY_BLOCK

SCALARS = pl.BlockSpec(memory_space=pltpu.SMEM)
ARRAY = pl.BlockSpec(memory_space=pltpu.VMEM)
LISTS = 3
TOGETHER = 8
UNROLL = 28
LB_BITS = 7
COUNTED = 8


def split(x):
    high = x.astype(BF16)
    return high, (x - high.astype(F32)).astype(BF16)


def stacked(x):
    return jnp.concatenate(split(x), axis=0)


def aligned(start, size, unit):
    return pl.ds(pl.multiple_of(start * unit, unit), size)


def stay(*arrays):
    return tuple(pltpu.with_memory_space_constraint(a, pltpu.HBM) for a in arrays)


REMAIN = pl.BlockSpec(memory_space=pltpu.HBM)


def fetch(given, local, arrived):
    copies = [pltpu.make_async_copy(a, b, arrived.at[i]) for i, (a, b) in enumerate(zip(given, local))]
    for copy in copies:
        copy.start()
    return copies


def listing_kernel(tile_total, *refs):
    given, (list_ref, total_ref, same_ref, wanted_ref, kept_ref) = refs[:5], refs[5:10]
    local, arrived = refs[10:15], refs[15]
    tiles_ref, count_ref, comm_ref, demand_ref, capacity_ref = local
    copies = fetch(given, local, arrived)
    blocks = tiles_ref.shape[0]
    spare = blocks * MAXT
    for copy in copies:
        copy.wait()

    def one_block(block, entry):
        live = count_ref[block]

        def one_pair(pair, entry):
            list_ref[0, entry] = block * MAXT + 2 * pair
            list_ref[1, entry] = tiles_ref[block, 2 * pair]
            list_ref[2, entry] = jnp.where(2 * pair + 1 < live, tiles_ref[block, 2 * pair + 1], tile_total)
            return entry + 1

        return lax.fori_loop(0, (live + 1) // 2, one_pair, entry)

    entries = lax.fori_loop(0, blocks, one_block, 0)
    batches = (entries + BATCH - 1) // BATCH
    total_ref[0] = batches
    total_ref[1] = (entries + COUNTED - 1) // COUNTED

    def pad(entry, carry):
        list_ref[0, entry] = spare
        list_ref[1, entry] = tile_total
        list_ref[2, entry] = tile_total
        return carry

    lax.fori_loop(entries, batches * BATCH, pad, 0)
    kept_ref[...] = capacity_ref[...]

    commodity_rows = lax.broadcasted_iota(jnp.int32, (LB, PATHS_PER_BLOCK), 0)
    for block in range(blocks):
        group, j = block // GROUP, block % GROUP
        demand = demand_ref[:, group * LB : (group + 1) * LB].astype(F32).astype(BF16)
        onehot = (commodity_rows == comm_ref[block : block + 1, :] + COMMODITY_BLOCK * j).astype(F32).astype(BF16)
        same = lax.dot_general(onehot, onehot, (((0,), (0,)), ((), ())), preferred_element_type=F32)
        same_ref[block] = same.astype(BF16)
        wanted_ref[block] = jnp.dot(demand, onehot, preferred_element_type=F32) * DEMAND_UNIT


def build_listing(tile_total, block_tiles, block_count, path_commodity, demand, capacity):
    blocks = block_tiles.shape[0]
    given = stay(block_tiles, block_count, path_commodity, demand, capacity.reshape(-1, LB))
    return pl.pallas_call(
        lambda *refs: listing_kernel(tile_total, *refs),
        in_specs=[REMAIN] * 5,
        out_specs=[SCALARS, SCALARS, ARRAY, ARRAY, ARRAY],
        out_shape=[
            jax.ShapeDtypeStruct((LISTS, blocks * MAXT // 2 + BATCH), jnp.int32),
            jax.ShapeDtypeStruct((2,), jnp.int32),
            jax.ShapeDtypeStruct((blocks, PATHS_PER_BLOCK, PATHS_PER_BLOCK), BF16),
            jax.ShapeDtypeStruct((blocks, demand.shape[0], PATHS_PER_BLOCK), F32),
            jax.ShapeDtypeStruct(given[4].shape, F32),
        ],
        scratch_shapes=[pltpu.SMEM(a.shape, a.dtype) for a in given[:2]]
        + [pltpu.VMEM(a.shape, a.dtype) for a in given[2:]]
        + [pltpu.SemaphoreType.DMA((5,))],
        compiler_params=pltpu.CompilerParams(vmem_limit_bytes=8 * MIB),
        cost_estimate=pl.CostEstimate(flops=10**9, bytes_accessed=10**7, transcendentals=0),
        name="listing",
    )(*given)


def incidence_kernel(list_ref, total_ref, given_ref, hits_ref, turned_ref, links_ref, arrived):
    copies = fetch([given_ref], [links_ref], arrived)
    blocks = links_ref.shape[1] // PATHS_PER_BLOCK
    for ref in (hits_ref, turned_ref):
        ref[-2 * LB :, :] = jnp.zeros((2 * LB, LB), BF16)
    lanes = [(lax.broadcasted_iota(jnp.int32, (PACK, LB), 0) + PACK * g).astype(F32).astype(BF16) for g in range(LB // PACK)]
    one, zero = jnp.ones((PACK, PATHS_PER_BLOCK), BF16), jnp.zeros((PACK, PATHS_PER_BLOCK), BF16)
    copies[0].wait()

    def count_step(step, carry):
        done = []
        for j in range(COUNTED):
            entry = step * COUNTED + j
            slot = list_ref[0, entry]
            block = jnp.minimum(slot // MAXT, blocks - 1)
            links = links_ref[:, aligned(block, PATHS_PER_BLOCK, PATHS_PER_BLOCK)]
            for side in range(2):
                place = (links - list_ref[1 + side, entry] * LB).astype(F32)
                counts = None
                for h in range(links.shape[0]):
                    row = jnp.broadcast_to(place[h : h + 1, :], (PACK, PATHS_PER_BLOCK)).astype(BF16)
                    hit = [jnp.where(row == lane, one, zero) for lane in lanes]
                    counts = hit if counts is None else [a + b for a, b in zip(counts, hit)]
                done.append((aligned(slot + side, LB, LB), jnp.concatenate(counts, axis=0)))
        for where, table in done:
            hits_ref[where, :] = table
            turned_ref[where, :] = table.T
        return carry

    lax.fori_loop(0, total_ref[1], count_step, 0)


def build_incidence(path_links, pairs, total):
    blocks = path_links.shape[1] // PATHS_PER_BLOCK
    slots = blocks * MAXT + 2
    return pl.pallas_call(
        incidence_kernel,
        in_specs=[SCALARS, SCALARS, REMAIN],
        out_specs=[ARRAY, ARRAY],
        out_shape=[
            jax.ShapeDtypeStruct((slots * LB, PATHS_PER_BLOCK), BF16),
            jax.ShapeDtypeStruct((slots * PATHS_PER_BLOCK, LB), BF16),
        ],
        scratch_shapes=[pltpu.VMEM(path_links.shape, path_links.dtype), pltpu.SemaphoreType.DMA((1,))],
        compiler_params=pltpu.CompilerParams(vmem_limit_bytes=8 * MIB),
        cost_estimate=pl.CostEstimate(flops=10**6, bytes_accessed=20 * 10**6, transcendentals=0),
        name="incidence",
    )(pairs, total, *stay(path_links))


def sweep(list_ref, total_ref, hits_ref, turned_ref, same_ref, wanted_at, put_flow, split_ref, cost_ref, flow_ref, load_ref):
    blocks, rows2 = same_ref.shape[0], cost_ref.shape[1]
    rows = rows2 // 2
    flow_ref[blocks] = jnp.zeros(flow_ref.shape[1:], BF16)
    split_ref[split_ref.shape[0] - 1] = jnp.zeros(split_ref.shape[1:], BF16)
    load_ref[...] = jnp.zeros_like(load_ref)
    cost_ref[...] = jnp.zeros_like(cost_ref)
    batches = total_ref[0]

    def cost_batch(batch, carry):
        done = []
        for j in range(BATCH):
            slot, left, right = (list_ref[i, batch * BATCH + j] for i in range(LISTS))
            block = slot // MAXT
            chosen = jnp.concatenate([split_ref[left], split_ref[right]], axis=1)
            done.append((block, jnp.dot(chosen, hits_ref[aligned(slot, 2 * LB, LB), :], preferred_element_type=F32)))
        for block, cost in done:
            cost_ref[block] += cost
        return carry

    lax.fori_loop(0, batches, cost_batch, 0)

    for block in range(blocks):
        weight = jnp.exp(-SOFTMIN_RATE * (cost_ref[block, :rows] + cost_ref[block, rows:]))
        total = jnp.dot(stacked(weight), same_ref[block], preferred_element_type=F32)
        flow = wanted_at(block) * weight / (total[:rows] + total[rows:])
        put_flow(block, flow)
        flow_ref[block] = stacked(flow)

    def load_batch(batch, carry):
        done = []
        for j in range(BATCH):
            slot, left, right = (list_ref[i, batch * BATCH + j] for i in range(LISTS))
            block = slot // MAXT
            for side, tile in enumerate((left, right)):
                turned = turned_ref[aligned(slot + side, LB, LB), :]
                done.append((tile, jnp.dot(flow_ref[block], turned, preferred_element_type=F32)))
        for tile, load in done:
            load_ref[tile] += load
        return carry

    lax.fori_loop(0, batches, load_batch, 0)


def spread(split_ref, first, shard):
    for k in range(shard.shape[-1] // LB):
        split_ref[first + k] = stacked(shard[:, k * LB : (k + 1) * LB])


def path_columns(block):
    return slice(block * PATHS_PER_BLOCK, (block + 1) * PATHS_PER_BLOCK)


def sweep_scratch(rows, tiles, blocks):
    return [
        pltpu.VMEM((tiles + 1, 2 * rows, LB), BF16),
        pltpu.VMEM((blocks + 1, 2 * rows, PATHS_PER_BLOCK), F32),
        pltpu.VMEM((blocks + 1, 2 * rows, PATHS_PER_BLOCK), BF16),
        pltpu.VMEM((tiles + 1, 2 * rows, LB), F32),
    ]


def sweep_cost(size):
    return pl.CostEstimate(flops=10**10, bytes_accessed=size, transcendentals=0)


def half_kernel(far, n, list_ref, total_ref, *refs):
    pieces, (hits_ref, turned_ref, same_ref, wanted_ref, capacity_ref) = refs[:n], refs[n : n + 5]
    flows_ref, mine_ref, other_ref, *scratch = refs[-7:]
    z = lax.axis_index("path")
    rows = scratch[0].shape[1] // 2
    side = lax.div(z, 2)
    side = 1 - side if far else side
    shard_tiles = pieces[0].shape[1] // LB
    for m, piece in enumerate(pieces):
        start = side if piece.shape[0] == 2 * rows else 0
        spread(scratch[0], (z ^ m) * shard_tiles, piece[aligned(start, rows, rows), :])

    def wanted_at(block):
        return wanted_ref[block, aligned(side, rows, rows), :]

    def put_flow(block, flow):
        flows_ref[:, path_columns(block)] = flow

    sweep(list_ref, total_ref, hits_ref, turned_ref, same_ref, wanted_at, put_flow, *scratch)
    load_ref = scratch[3]
    height = rows // 2
    for out_ref, place in ((mine_ref, lax.rem(z, 2)), (other_ref, 1 - lax.rem(z, 2))):
        for k in range(load_ref.shape[0] - 1):
            high = load_ref[k, aligned(place, height, height), :]
            out_ref[k] = high + load_ref[k, pl.ds(pl.multiple_of(rows + place * height, height), height), :]
    for out_ref, start in ((mine_ref, 0), (other_ref, height // 2 if far else 0)):
        out_ref[load_ref.shape[0] - 1] = jnp.zeros((height, LB), F32)
        out_ref[load_ref.shape[0] - 1, start : start + shard_tiles, :] = capacity_ref[...]


def half_sweep(pieces, rows, built, capacity, far):
    hits, turned, pairs, total, same, wanted = built
    own = pieces[0].shape[1]
    n = len(pieces)
    blocks = wanted.shape[0]
    tiles = n * own // LB
    return pl.pallas_call(
        lambda *refs: half_kernel(far, n, *refs),
        in_specs=[SCALARS, SCALARS] + [ARRAY] * (n + 5),
        out_specs=[ARRAY] * 3,
        out_shape=[jax.ShapeDtypeStruct((rows, blocks * PATHS_PER_BLOCK), F32)]
        + [jax.ShapeDtypeStruct((tiles + 1, rows // 2, LB), F32)] * 2,
        scratch_shapes=sweep_scratch(rows, tiles, blocks),
        compiler_params=pltpu.CompilerParams(vmem_limit_bytes=16 * MIB),
        cost_estimate=sweep_cost(25 * 10**6),
        name="far_sweep" if far else "near_sweep",
    )(pairs, total, *pieces, hits, turned, same, wanted, capacity)


def wide_kernel(list_ref, total_ref, lengths_ref, hits_ref, turned_ref, same_ref, wanted_ref, flows_ref, out_ref, *scratch):
    shards, _, own = lengths_ref.shape
    rows = lengths_ref.shape[1]

    def one_shard(i, carry):
        spread(scratch[0], i * (own // LB), lengths_ref[i])
        return carry

    lax.fori_loop(0, shards, one_shard, 0)

    def put_flow(block, flow):
        flows_ref[:, path_columns(block)] = flow

    sweep(
        list_ref, total_ref, hits_ref, turned_ref, same_ref, lambda block: wanted_ref[block], put_flow, *scratch
    )
    out_ref[...] = scratch[3][:-1, :rows, :] + scratch[3][:-1, rows:, :]


def wide_sweep(lengths, built):
    hits, turned, pairs, total, same, wanted = built
    shards, rows, own = lengths.shape
    blocks = wanted.shape[0]
    tiles = shards * own // LB
    return pl.pallas_call(
        wide_kernel,
        in_specs=[SCALARS, SCALARS] + [ARRAY] * 5,
        out_specs=[ARRAY] * 2,
        out_shape=[
            jax.ShapeDtypeStruct((rows, blocks * PATHS_PER_BLOCK), F32),
            jax.ShapeDtypeStruct((tiles, rows, LB), F32),
        ],
        scratch_shapes=sweep_scratch(rows, tiles, blocks),
        compiler_params=pltpu.CompilerParams(vmem_limit_bytes=48 * MIB),
        cost_estimate=sweep_cost(10**7),
        name="wide_sweep",
    )(pairs, total, lengths, hits, turned, same, wanted)


def growth_kernel(n, parts, *refs):
    lengths, (capacity_ref, weight_ref) = refs[:n], refs[n : n + 2]
    loads = refs[n + 2 : n + 2 + parts]
    next_refs, mixed_ref, grown_ref = refs[-n - 2 : -2], refs[-2], refs[-1]
    z = lax.axis_index("path")
    links_total, height, _ = grown_ref.shape
    shard_tiles = links_total // n
    total = jnp.zeros((height, LB), F32)
    own, near, far = capacity_ref[...], loads[1][links_total], loads[2][links_total]
    capacities = (own, near, far, far[height // 2 :])
    for m in range(n):
        row = aligned(z if lengths[m].shape[0] == n * height else lax.rem(z, 2), height, height)
        first = (z ^ m) * shard_tiles
        for k in range(shard_tiles):
            columns = slice(k * LB, (k + 1) * LB)
            load = loads[0][first + k]
            for ref in loads[1:]:
                load = load + ref[first + k]
            grown = lengths[m][row, columns] * jnp.exp(STEP_RATE * load / capacities[m][k : k + 1])
            grown_ref[m * shard_tiles + k] = grown
            total = total + grown
    factor = (links_total * LB) / jnp.sum(total, axis=1, keepdims=True)
    weight = weight_ref[aligned(z, height, height), :]
    for m in range(n):
        first = (z ^ m) * shard_tiles
        for k in range(shard_tiles):
            new = grown_ref[m * shard_tiles + k] * factor
            next_refs[m][:, k * LB : (k + 1) * LB] = new
            mixed_ref[pl.ds(first + k, 1), :] = jnp.sum(weight * new, axis=0, keepdims=True)


def grow(loads, lengths, capacity, weights):
    n, parts = len(lengths), len(loads)
    tiles, height = loads[0].shape[0] - 1, loads[0].shape[1]
    return pl.pallas_call(
        lambda *refs: growth_kernel(n, parts, *refs),
        in_specs=[ARRAY] * (n + 2 + parts),
        out_specs=[ARRAY] * (n + 1),
        out_shape=[jax.ShapeDtypeStruct((height, tiles * LB // n), F32)] * n + [jax.ShapeDtypeStruct((tiles, LB), F32)],
        scratch_shapes=[pltpu.VMEM((tiles, height, LB), F32)],
        compiler_params=pltpu.CompilerParams(vmem_limit_bytes=8 * MIB),
        cost_estimate=pl.CostEstimate(flops=10**6, bytes_accessed=5 * 10**6, transcendentals=10**5),
        name="growth",
    )(*lengths, capacity, weights, *loads)


def robust_kernel(parts, links_ref, *refs):
    part_refs, (out_ref, mixed_ref) = refs[:parts], refs[parts:]
    blocks = out_ref.shape[0]
    hops = links_ref.shape[0]
    mixed = part_refs[0][...]
    for ref in part_refs[1:]:
        mixed = mixed + ref[...]
    mixed_ref[...] = mixed
    for first in range(0, blocks, TOGETHER):
        group = range(first, min(first + TOGETHER, blocks))
        links = [links_ref[:, path_columns(block)] for block in group]

        def one_tile(tile, costs):
            table = jnp.broadcast_to(mixed_ref[pl.ds(tile, 1), :], (hops, LB))
            found = [jnp.take_along_axis(table, x & (LB - 1), axis=1) for x in links]
            return [jnp.where((x >> LB_BITS) == tile, f, c) for x, f, c in zip(links, found, costs)]

        tiles = mixed_ref.shape[0]
        costs = [jnp.zeros((hops, PATHS_PER_BLOCK), F32)] * len(links)
        step = UNROLL if tiles % UNROLL == 0 else 1

        def some_tiles(i, costs):
            for j in range(step):
                costs = one_tile(i * step + j, costs)
            return costs

        costs = lax.fori_loop(0, tiles // step, some_tiles, costs)
        for block, cost in zip(group, costs):
            out_ref[block : block + 1, :] = jnp.sum(cost, axis=0, keepdims=True) / S


def robust_costs(path_links, parts):
    hops, paths = path_links.shape
    blocks = paths // PATHS_PER_BLOCK
    out = pl.pallas_call(
        lambda *refs: robust_kernel(len(parts), *refs),
        in_specs=[ARRAY] * (len(parts) + 1),
        out_specs=ARRAY,
        out_shape=jax.ShapeDtypeStruct((blocks, PATHS_PER_BLOCK), F32),
        scratch_shapes=[pltpu.VMEM(parts[0].shape, F32)],
        compiler_params=pltpu.CompilerParams(vmem_limit_bytes=8 * MIB),
        cost_estimate=pl.CostEstimate(flops=10**6, bytes_accessed=10**6, transcendentals=0),
        name="robust",
    )(path_links, *parts)
    return out.reshape(-1)


def exchange(x, axis, n, bit):
    return lax.ppermute(x, axis, [(i, i ^ bit) for i in range(n)])


def body_paired(sizes, path_links, block_tiles, block_count, path_commodity, demand, lengths, capacity, scenario_weight):
    n = sizes["path"]
    rows, own = lengths.shape
    half, height = rows // 2, rows // n
    z = lax.axis_index("path").astype(jnp.int32)
    side = z // 2
    far = lax.dynamic_slice(lengths, ((1 - side) * half, 0), (half, own))
    near = lax.dynamic_slice(lengths, (side * half, 0), (half, own))

    def swap(x, m):
        return exchange(x, "path", n, m)

    near_straight, near_crossed = swap(near, 2), swap(near, 3)
    pairs, total, same, wanted, capacity_tiles = build_listing(
        n * own // LB, block_tiles, block_count, path_commodity, demand, capacity
    )
    late, same = lax.optimization_barrier((far, same))
    shared = swap(lengths, 1)
    far_pieces = [far, shared, near_straight, near_crossed]
    near_pieces = [near, shared, swap(late, 2), swap(late, 3)]
    built = (*build_incidence(path_links, pairs, total), pairs, total, same, wanted)
    far_flows, straight, crossed = half_sweep(far_pieces, half, built, capacity_tiles, True)
    partial = straight + swap(crossed, 1)
    near_flows, mine, other = half_sweep(near_pieces, half, built, capacity_tiles, False)
    partial, other, near_flows = lax.optimization_barrier((partial, other, near_flows))
    loads = [mine, swap(other, 1), swap(partial, 2)]
    first, second = jnp.where(side == 0, near_flows, far_flows), jnp.where(side == 0, far_flows, near_flows)
    flows = jnp.concatenate([first, second], axis=0)
    weight_column = scenario_weight[:, None]
    flows, weight_column = lax.optimization_barrier((flows, weight_column))
    *new, mixed = grow(loads, near_pieces, capacity_tiles, weight_column)
    mixed = mixed + exchange(mixed, "sub", 2, 1)
    mixed = mixed + exchange(mixed, "scen", 2, 1)
    mixed = mixed + swap(mixed, 1)
    parts = [mixed, swap(mixed, 2)]
    arrived = [new[0]] + [swap(new[m], m) for m in range(1, n)]
    lengths_next = jnp.zeros((rows, own), F32)
    for m in range(n):
        lengths_next = lax.dynamic_update_slice(lengths_next, arrived[m], ((z ^ m) * height, 0))
    parts[1], lengths_next = lax.optimization_barrier((parts[1], lengths_next))
    robust = robust_costs(path_links, parts)
    return flows, lengths_next, robust


def body_wide(sizes, path_links, block_tiles, block_count, path_commodity, demand, lengths, capacity, scenario_weight):
    gathered = lax.all_gather(lengths, "path", axis=0, tiled=False)
    tiles = gathered.shape[0] * gathered.shape[2] // LB
    pairs, total, same, wanted, _ = build_listing(tiles, block_tiles, block_count, path_commodity, demand, capacity)
    built = (*build_incidence(path_links, pairs, total), pairs, total, same, wanted)
    flows, loads = wide_sweep(gathered, built)
    loads = loads.transpose(1, 0, 2).reshape(lengths.shape[0], -1)
    own_loads = lax.psum_scatter(loads, "path", scatter_dimension=1, tiled=True)
    grown = lengths * jnp.exp(STEP_RATE * own_loads / capacity[None, :])
    totals = lax.psum(jnp.sum(grown, axis=1), "path")
    lengths_next = grown * (loads.shape[1] / totals)[:, None]
    mixed = lax.psum(jnp.sum(lengths_next * scenario_weight[:, None], axis=0), ("scen", "sub"))
    mixed = lax.all_gather(mixed.reshape(-1, LB), "path", axis=0, tiled=True)
    return flows, lengths_next, robust_costs(path_links, [mixed])


def solution(mesh):
    sizes = dict(mesh.shape)

    def body(*args):
        paired = sizes["path"] == 4 and sizes["scen"] == 2 and sizes["sub"] == 2 and args[5].shape[0] % 64 == 0 and args[5].shape[1] // LB <= args[5].shape[0] // 8
        return (body_paired if paired else body_wide)(sizes, *args)

    return jax.shard_map(
        body,
        mesh=mesh,
        in_specs=(
            P(None, ("grp", "path")),
            P(("grp", "path"), None),
            P(("grp", "path")),
            P(("grp", "path"), None),
            P(("scen", "sub"), ("grp", "path")),
            P(("scen", "sub"), ("grp", "path")),
            P(("grp", "path")),
            P(("grp", "scen", "sub")),
        ),
        out_specs=(
            P(("scen", "sub"), ("grp", "path")),
            P(("scen", "sub"), ("grp", "path")),
            P(("grp", "path")),
        ),
        check_vma=False,
    )
```

```python
import jax
import jax.numpy as jnp
from jax import lax
from jax.experimental import pallas as pl
from jax.experimental.pallas import tpu as pltpu
from jax.sharding import PartitionSpec as P

PATHS_PER_BLOCK = 128
LB = 128
MAXT = 16
COMMODITY_BLOCK = 32
S = 256

SOFTMIN_RATE = 0.25
STEP_RATE = 1.0
DEMAND_UNIT = 0.0625
MIB = 1024 * 1024

F32 = jnp.float32
BF16 = jnp.bfloat16
PACK = 16
BATCH = 16
GROUP = LB // COMMODITY_BLOCK

SCALARS = pl.BlockSpec(memory_space=pltpu.SMEM)
ARRAY = pl.BlockSpec(memory_space=pltpu.VMEM)
LISTS = 3
TOGETHER = 8
UNROLL = 28
LB_BITS = 7
COUNTED = 8


def split(x):
    high = x.astype(BF16)
    return high, (x - high.astype(F32)).astype(BF16)


def stacked(x):
    return jnp.concatenate(split(x), axis=0)


def aligned(start, size, unit):
    return pl.ds(pl.multiple_of(start * unit, unit), size)


def stay(*arrays):
    return tuple(pltpu.with_memory_space_constraint(a, pltpu.HBM) for a in arrays)


REMAIN = pl.BlockSpec(memory_space=pltpu.HBM)


def fetch(given, local, arrived):
    copies = [pltpu.make_async_copy(a, b, arrived.at[i]) for i, (a, b) in enumerate(zip(given, local))]
    for copy in copies:
        copy.start()
    return copies


def listing_kernel(tile_total, *refs):
    given, (list_ref, total_ref, same_ref, wanted_ref, kept_ref) = refs[:5], refs[5:10]
    local, arrived = refs[10:15], refs[15]
    tiles_ref, count_ref, comm_ref, demand_ref, capacity_ref = local
    copies = fetch(given, local, arrived)
    blocks = tiles_ref.shape[0]
    spare = blocks * MAXT
    for copy in copies:
        copy.wait()

    def one_block(block, entry):
        live = count_ref[block]

        def one_pair(pair, entry):
            list_ref[0, entry] = block * MAXT + 2 * pair
            list_ref[1, entry] = tiles_ref[block, 2 * pair]
            list_ref[2, entry] = jnp.where(2 * pair + 1 < live, tiles_ref[block, 2 * pair + 1], tile_total)
            return entry + 1

        return lax.fori_loop(0, (live + 1) // 2, one_pair, entry)

    entries = lax.fori_loop(0, blocks, one_block, 0)
    batches = (entries + BATCH - 1) // BATCH
    total_ref[0] = batches
    total_ref[1] = (entries + COUNTED - 1) // COUNTED

    def pad(entry, carry):
        list_ref[0, entry] = spare
        list_ref[1, entry] = tile_total
        list_ref[2, entry] = tile_total
        return carry

    lax.fori_loop(entries, batches * BATCH, pad, 0)
    kept_ref[...] = capacity_ref[...]

    commodity_rows = lax.broadcasted_iota(jnp.int32, (LB, PATHS_PER_BLOCK), 0)
    for block in range(blocks):
        group, j = block // GROUP, block % GROUP
        demand = demand_ref[:, group * LB : (group + 1) * LB].astype(F32).astype(BF16)
        onehot = (commodity_rows == comm_ref[block : block + 1, :] + COMMODITY_BLOCK * j).astype(F32).astype(BF16)
        same = lax.dot_general(onehot, onehot, (((0,), (0,)), ((), ())), preferred_element_type=F32)
        same_ref[block] = same.astype(BF16)
        wanted_ref[block] = jnp.dot(demand, onehot, preferred_element_type=F32) * DEMAND_UNIT


def build_listing(tile_total, block_tiles, block_count, path_commodity, demand, capacity):
    blocks = block_tiles.shape[0]
    given = stay(block_tiles, block_count, path_commodity, demand, capacity.reshape(-1, LB))
    return pl.pallas_call(
        lambda *refs: listing_kernel(tile_total, *refs),
        in_specs=[REMAIN] * 5,
        out_specs=[SCALARS, SCALARS, ARRAY, ARRAY, ARRAY],
        out_shape=[
            jax.ShapeDtypeStruct((LISTS, blocks * MAXT // 2 + BATCH), jnp.int32),
            jax.ShapeDtypeStruct((2,), jnp.int32),
            jax.ShapeDtypeStruct((blocks, PATHS_PER_BLOCK, PATHS_PER_BLOCK), BF16),
            jax.ShapeDtypeStruct((blocks, demand.shape[0], PATHS_PER_BLOCK), F32),
            jax.ShapeDtypeStruct(given[4].shape, F32),
        ],
        scratch_shapes=[pltpu.SMEM(a.shape, a.dtype) for a in given[:2]]
        + [pltpu.VMEM(a.shape, a.dtype) for a in given[2:]]
        + [pltpu.SemaphoreType.DMA((5,))],
        compiler_params=pltpu.CompilerParams(vmem_limit_bytes=8 * MIB),
        cost_estimate=pl.CostEstimate(flops=10**9, bytes_accessed=10**7, transcendentals=0),
        name="listing",
    )(*given)


def incidence_kernel(list_ref, total_ref, given_ref, hits_ref, turned_ref, links_ref, arrived):
    copies = fetch([given_ref], [links_ref], arrived)
    blocks = links_ref.shape[1] // PATHS_PER_BLOCK
    for ref in (hits_ref, turned_ref):
        ref[-2 * LB :, :] = jnp.zeros((2 * LB, LB), BF16)
    lanes = [(lax.broadcasted_iota(jnp.int32, (PACK, LB), 0) + PACK * g).astype(F32).astype(BF16) for g in range(LB // PACK)]
    one, zero = jnp.ones((PACK, PATHS_PER_BLOCK), BF16), jnp.zeros((PACK, PATHS_PER_BLOCK), BF16)
    copies[0].wait()

    def count_step(step, carry):
        done = []
        for j in range(COUNTED):
            entry = step * COUNTED + j
            slot = list_ref[0, entry]
            block = jnp.minimum(slot // MAXT, blocks - 1)
            links = links_ref[:, aligned(block, PATHS_PER_BLOCK, PATHS_PER_BLOCK)]
            for side in range(2):
                place = (links - list_ref[1 + side, entry] * LB).astype(F32)
                counts = None
                for h in range(links.shape[0]):
                    row = jnp.broadcast_to(place[h : h + 1, :], (PACK, PATHS_PER_BLOCK)).astype(BF16)
                    hit = [jnp.where(row == lane, one, zero) for lane in lanes]
                    counts = hit if counts is None else [a + b for a, b in zip(counts, hit)]
                done.append((aligned(slot + side, LB, LB), jnp.concatenate(counts, axis=0)))
        for where, table in done:
            hits_ref[where, :] = table
            turned_ref[where, :] = table.T
        return carry

    lax.fori_loop(0, total_ref[1], count_step, 0)


def build_incidence(path_links, pairs, total):
    blocks = path_links.shape[1] // PATHS_PER_BLOCK
    slots = blocks * MAXT + 2
    return pl.pallas_call(
        incidence_kernel,
        in_specs=[SCALARS, SCALARS, REMAIN],
        out_specs=[ARRAY, ARRAY],
        out_shape=[
            jax.ShapeDtypeStruct((slots * LB, PATHS_PER_BLOCK), BF16),
            jax.ShapeDtypeStruct((slots * PATHS_PER_BLOCK, LB), BF16),
        ],
        scratch_shapes=[pltpu.VMEM(path_links.shape, path_links.dtype), pltpu.SemaphoreType.DMA((1,))],
        compiler_params=pltpu.CompilerParams(vmem_limit_bytes=8 * MIB),
        cost_estimate=pl.CostEstimate(flops=10**6, bytes_accessed=20 * 10**6, transcendentals=0),
        name="incidence",
    )(pairs, total, *stay(path_links))


def sweep(list_ref, total_ref, hits_ref, turned_ref, same_ref, wanted_at, put_flow, split_ref, cost_ref, flow_ref, load_ref):
    blocks, rows2 = same_ref.shape[0], cost_ref.shape[1]
    rows = rows2 // 2
    flow_ref[blocks] = jnp.zeros(flow_ref.shape[1:], BF16)
    split_ref[split_ref.shape[0] - 1] = jnp.zeros(split_ref.shape[1:], BF16)
    load_ref[...] = jnp.zeros_like(load_ref)
    cost_ref[...] = jnp.zeros_like(cost_ref)
    batches = total_ref[0]

    def cost_batch(batch, carry):
        done = []
        for j in range(BATCH):
            slot, left, right = (list_ref[i, batch * BATCH + j] for i in range(LISTS))
            block = slot // MAXT
            chosen = jnp.concatenate([split_ref[left], split_ref[right]], axis=1)
            done.append((block, jnp.dot(chosen, hits_ref[aligned(slot, 2 * LB, LB), :], preferred_element_type=F32)))
        for block, cost in done:
            cost_ref[block] += cost
        return carry

    lax.fori_loop(0, batches, cost_batch, 0)

    for block in range(blocks):
        weight = jnp.exp(-SOFTMIN_RATE * (cost_ref[block, :rows] + cost_ref[block, rows:]))
        total = jnp.dot(stacked(weight), same_ref[block], preferred_element_type=F32)
        flow = wanted_at(block) * weight / (total[:rows] + total[rows:])
        put_flow(block, flow)
        flow_ref[block] = stacked(flow)

    def load_batch(batch, carry):
        done = []
        for j in range(BATCH):
            slot, left, right = (list_ref[i, batch * BATCH + j] for i in range(LISTS))
            block = slot // MAXT
            for side, tile in enumerate((left, right)):
                turned = turned_ref[aligned(slot + side, LB, LB), :]
                done.append((tile, jnp.dot(flow_ref[block], turned, preferred_element_type=F32)))
        for tile, load in done:
            load_ref[tile] += load
        return carry

    lax.fori_loop(0, batches, load_batch, 0)


def spread(split_ref, first, shard):
    for k in range(shard.shape[-1] // LB):
        split_ref[first + k] = stacked(shard[:, k * LB : (k + 1) * LB])


def path_columns(block):
    return slice(block * PATHS_PER_BLOCK, (block + 1) * PATHS_PER_BLOCK)


def sweep_scratch(rows, tiles, blocks):
    return [
        pltpu.VMEM((tiles + 1, 2 * rows, LB), BF16),
        pltpu.VMEM((blocks + 1, 2 * rows, PATHS_PER_BLOCK), F32),
        pltpu.VMEM((blocks + 1, 2 * rows, PATHS_PER_BLOCK), BF16),
        pltpu.VMEM((tiles + 1, 2 * rows, LB), F32),
    ]


def sweep_cost(size):
    return pl.CostEstimate(flops=10**10, bytes_accessed=size, transcendentals=0)


def half_kernel(far, n, list_ref, total_ref, *refs):
    pieces, (hits_ref, turned_ref, same_ref, wanted_ref, capacity_ref) = refs[:n], refs[n : n + 5]
    flows_ref, mine_ref, other_ref, *scratch = refs[-7:]
    z = lax.axis_index("path")
    rows = scratch[0].shape[1] // 2
    side = lax.div(z, 2)
    side = 1 - side if far else side
    shard_tiles = pieces[0].shape[1] // LB
    for m, piece in enumerate(pieces):
        start = side if piece.shape[0] == 2 * rows else 0
        spread(scratch[0], (z ^ m) * shard_tiles, piece[aligned(start, rows, rows), :])

    def wanted_at(block):
        return wanted_ref[block, aligned(side, rows, rows), :]

    def put_flow(block, flow):
        flows_ref[:, path_columns(block)] = flow

    sweep(list_ref, total_ref, hits_ref, turned_ref, same_ref, wanted_at, put_flow, *scratch)
    load_ref = scratch[3]
    height = rows // 2
    for out_ref, place in ((mine_ref, lax.rem(z, 2)), (other_ref, 1 - lax.rem(z, 2))):
        for k in range(load_ref.shape[0] - 1):
            high = load_ref[k, aligned(place, height, height), :]
            out_ref[k] = high + load_ref[k, pl.ds(pl.multiple_of(rows + place * height, height), height), :]
    for out_ref, start in ((mine_ref, 0), (other_ref, height // 2 if far else 0)):
        out_ref[load_ref.shape[0] - 1] = jnp.zeros((height, LB), F32)
        out_ref[load_ref.shape[0] - 1, start : start + shard_tiles, :] = capacity_ref[...]


def half_sweep(pieces, rows, built, capacity, far):
    hits, turned, pairs, total, same, wanted = built
    own = pieces[0].shape[1]
    n = len(pieces)
    blocks = wanted.shape[0]
    tiles = n * own // LB
    return pl.pallas_call(
        lambda *refs: half_kernel(far, n, *refs),
        in_specs=[SCALARS, SCALARS] + [ARRAY] * (n + 5),
        out_specs=[ARRAY] * 3,
        out_shape=[jax.ShapeDtypeStruct((rows, blocks * PATHS_PER_BLOCK), F32)]
        + [jax.ShapeDtypeStruct((tiles + 1, rows // 2, LB), F32)] * 2,
        scratch_shapes=sweep_scratch(rows, tiles, blocks),
        compiler_params=pltpu.CompilerParams(vmem_limit_bytes=16 * MIB),
        cost_estimate=sweep_cost(25 * 10**6),
        name="far_sweep" if far else "near_sweep",
    )(pairs, total, *pieces, hits, turned, same, wanted, capacity)


def wide_kernel(list_ref, total_ref, lengths_ref, hits_ref, turned_ref, same_ref, wanted_ref, flows_ref, out_ref, *scratch):
    shards, _, own = lengths_ref.shape
    rows = lengths_ref.shape[1]

    def one_shard(i, carry):
        spread(scratch[0], i * (own // LB), lengths_ref[i])
        return carry

    lax.fori_loop(0, shards, one_shard, 0)

    def put_flow(block, flow):
        flows_ref[:, path_columns(block)] = flow

    sweep(
        list_ref, total_ref, hits_ref, turned_ref, same_ref, lambda block: wanted_ref[block], put_flow, *scratch
    )
    out_ref[...] = scratch[3][:-1, :rows, :] + scratch[3][:-1, rows:, :]


def wide_sweep(lengths, built):
    hits, turned, pairs, total, same, wanted = built
    shards, rows, own = lengths.shape
    blocks = wanted.shape[0]
    tiles = shards * own // LB
    return pl.pallas_call(
        wide_kernel,
        in_specs=[SCALARS, SCALARS] + [ARRAY] * 5,
        out_specs=[ARRAY] * 2,
        out_shape=[
            jax.ShapeDtypeStruct((rows, blocks * PATHS_PER_BLOCK), F32),
            jax.ShapeDtypeStruct((tiles, rows, LB), F32),
        ],
        scratch_shapes=sweep_scratch(rows, tiles, blocks),
        compiler_params=pltpu.CompilerParams(vmem_limit_bytes=48 * MIB),
        cost_estimate=sweep_cost(10**7),
        name="wide_sweep",
    )(pairs, total, lengths, hits, turned, same, wanted)


def growth_kernel(n, parts, *refs):
    lengths, (capacity_ref, weight_ref) = refs[:n], refs[n : n + 2]
    loads = refs[n + 2 : n + 2 + parts]
    next_refs, mixed_ref, grown_ref = refs[-n - 2 : -2], refs[-2], refs[-1]
    z = lax.axis_index("path")
    links_total, height, _ = grown_ref.shape
    shard_tiles = links_total // n
    total = jnp.zeros((height, LB), F32)
    own, near, far = capacity_ref[...], loads[1][links_total], loads[2][links_total]
    capacities = (own, near, far, far[height // 2 :])
    for m in range(n):
        row = aligned(z if lengths[m].shape[0] == n * height else lax.rem(z, 2), height, height)
        first = (z ^ m) * shard_tiles
        for k in range(shard_tiles):
            columns = slice(k * LB, (k + 1) * LB)
            load = loads[0][first + k]
            for ref in loads[1:]:
                load = load + ref[first + k]
            grown = lengths[m][row, columns] * jnp.exp(STEP_RATE * load / capacities[m][k : k + 1])
            grown_ref[m * shard_tiles + k] = grown
            total = total + grown
    factor = (links_total * LB) / jnp.sum(total, axis=1, keepdims=True)
    weight = weight_ref[aligned(z, height, height), :]
    for m in range(n):
        first = (z ^ m) * shard_tiles
        for k in range(shard_tiles):
            new = grown_ref[m * shard_tiles + k] * factor
            next_refs[m][:, k * LB : (k + 1) * LB] = new
            mixed_ref[pl.ds(first + k, 1), :] = jnp.sum(weight * new, axis=0, keepdims=True)


def grow(loads, lengths, capacity, weights):
    n, parts = len(lengths), len(loads)
    tiles, height = loads[0].shape[0] - 1, loads[0].shape[1]
    return pl.pallas_call(
        lambda *refs: growth_kernel(n, parts, *refs),
        in_specs=[ARRAY] * (n + 2 + parts),
        out_specs=[ARRAY] * (n + 1),
        out_shape=[jax.ShapeDtypeStruct((height, tiles * LB // n), F32)] * n + [jax.ShapeDtypeStruct((tiles, LB), F32)],
        scratch_shapes=[pltpu.VMEM((tiles, height, LB), F32)],
        compiler_params=pltpu.CompilerParams(vmem_limit_bytes=8 * MIB),
        cost_estimate=pl.CostEstimate(flops=10**6, bytes_accessed=5 * 10**6, transcendentals=10**5),
        name="growth",
    )(*lengths, capacity, weights, *loads)


def robust_kernel(parts, links_ref, *refs):
    part_refs, (out_ref, mixed_ref) = refs[:parts], refs[parts:]
    blocks = out_ref.shape[0]
    hops = links_ref.shape[0]
    mixed = part_refs[0][...]
    for ref in part_refs[1:]:
        mixed = mixed + ref[...]
    mixed_ref[...] = mixed
    for first in range(0, blocks, TOGETHER):
        group = range(first, min(first + TOGETHER, blocks))
        links = [links_ref[:, path_columns(block)] for block in group]

        def one_tile(tile, costs):
            table = jnp.broadcast_to(mixed_ref[pl.ds(tile, 1), :], (hops, LB))
            found = [jnp.take_along_axis(table, x & (LB - 1), axis=1) for x in links]
            return [jnp.where((x >> LB_BITS) == tile, f, c) for x, f, c in zip(links, found, costs)]

        tiles = mixed_ref.shape[0]
        costs = [jnp.zeros((hops, PATHS_PER_BLOCK), F32)] * len(links)
        step = UNROLL if tiles % UNROLL == 0 else 1

        def some_tiles(i, costs):
            for j in range(step):
                costs = one_tile(i * step + j, costs)
            return costs

        costs = lax.fori_loop(0, tiles // step, some_tiles, costs)
        for block, cost in zip(group, costs):
            out_ref[block : block + 1, :] = jnp.sum(cost, axis=0, keepdims=True) / S


def robust_costs(path_links, parts):
    hops, paths = path_links.shape
    blocks = paths // PATHS_PER_BLOCK
    out = pl.pallas_call(
        lambda *refs: robust_kernel(len(parts), *refs),
        in_specs=[ARRAY] * (len(parts) + 1),
        out_specs=ARRAY,
        out_shape=jax.ShapeDtypeStruct((blocks, PATHS_PER_BLOCK), F32),
        scratch_shapes=[pltpu.VMEM(parts[0].shape, F32)],
        compiler_params=pltpu.CompilerParams(vmem_limit_bytes=8 * MIB),
        cost_estimate=pl.CostEstimate(flops=10**6, bytes_accessed=10**6, transcendentals=0),
        name="robust",
    )(path_links, *parts)
    return out.reshape(-1)


def exchange(x, axis, n, bit):
    return lax.ppermute(x, axis, [(i, i ^ bit) for i in range(n)])


def body_paired(sizes, path_links, block_tiles, block_count, path_commodity, demand, lengths, capacity, scenario_weight):
    n = sizes["path"]
    rows, own = lengths.shape
    half, height = rows // 2, rows // n
    z = lax.axis_index("path").astype(jnp.int32)
    side = z // 2
    far = lax.dynamic_slice(lengths, ((1 - side) * half, 0), (half, own))
    near = lax.dynamic_slice(lengths, (side * half, 0), (half, own))

    def swap(x, m):
        return exchange(x, "path", n, m)

    near_straight, near_crossed = swap(near, 2), swap(near, 3)
    pairs, total, same, wanted, capacity_tiles = build_listing(
        n * own // LB, block_tiles, block_count, path_commodity, demand, capacity
    )
    late, same = lax.optimization_barrier((far, same))
    shared = swap(lengths, 1)
    far_pieces = [far, shared, near_straight, near_crossed]
    near_pieces = [near, shared, swap(late, 2), swap(late, 3)]
    built = (*build_incidence(path_links, pairs, total), pairs, total, same, wanted)
    far_flows, straight, crossed = half_sweep(far_pieces, half, built, capacity_tiles, True)
    partial = straight + swap(crossed, 1)
    near_flows, mine, other = half_sweep(near_pieces, half, built, capacity_tiles, False)
    partial, other, near_flows = lax.optimization_barrier((partial, other, near_flows))
    loads = [mine, swap(other, 1), swap(partial, 2)]
    first, second = jnp.where(side == 0, near_flows, far_flows), jnp.where(side == 0, far_flows, near_flows)
    flows = jnp.concatenate([first, second], axis=0)
    weight_column = scenario_weight[:, None]
    flows, weight_column = lax.optimization_barrier((flows, weight_column))
    *new, mixed = grow(loads, near_pieces, capacity_tiles, weight_column)
    mixed = mixed + exchange(mixed, "sub", 2, 1)
    mixed, *new[1:] = lax.optimization_barrier((mixed, *new[1:]))
    diagonal = exchange(mixed, ("path", "scen"), 2 * n, 3)
    mixed = mixed + exchange(mixed, "scen", 2, 1) + swap(mixed, 1) + diagonal
    parts = [mixed, swap(mixed, 2)]
    arrived = [new[0]] + [swap(new[m], m) for m in range(1, n)]
    lengths_next = jnp.zeros((rows, own), F32)
    for m in range(n):
        lengths_next = lax.dynamic_update_slice(lengths_next, arrived[m], ((z ^ m) * height, 0))
    parts[1], lengths_next = lax.optimization_barrier((parts[1], lengths_next))
    robust = robust_costs(path_links, parts)
    return flows, lengths_next, robust


def body_wide(sizes, path_links, block_tiles, block_count, path_commodity, demand, lengths, capacity, scenario_weight):
    gathered = lax.all_gather(lengths, "path", axis=0, tiled=False)
    tiles = gathered.shape[0] * gathered.shape[2] // LB
    pairs, total, same, wanted, _ = build_listing(tiles, block_tiles, block_count, path_commodity, demand, capacity)
    built = (*build_incidence(path_links, pairs, total), pairs, total, same, wanted)
    flows, loads = wide_sweep(gathered, built)
    loads = loads.transpose(1, 0, 2).reshape(lengths.shape[0], -1)
    own_loads = lax.psum_scatter(loads, "path", scatter_dimension=1, tiled=True)
    grown = lengths * jnp.exp(STEP_RATE * own_loads / capacity[None, :])
    totals = lax.psum(jnp.sum(grown, axis=1), "path")
    lengths_next = grown * (loads.shape[1] / totals)[:, None]
    mixed = lax.psum(jnp.sum(lengths_next * scenario_weight[:, None], axis=0), ("scen", "sub"))
    mixed = lax.all_gather(mixed.reshape(-1, LB), "path", axis=0, tiled=True)
    return flows, lengths_next, robust_costs(path_links, [mixed])


def solution(mesh):
    sizes = dict(mesh.shape)

    def body(*args):
        paired = sizes["path"] == 4 and sizes["scen"] == 2 and sizes["sub"] == 2 and args[5].shape[0] % 64 == 0 and args[5].shape[1] // LB <= args[5].shape[0] // 8
        return (body_paired if paired else body_wide)(sizes, *args)

    return jax.shard_map(
        body,
        mesh=mesh,
        in_specs=(
            P(None, ("grp", "path")),
            P(("grp", "path"), None),
            P(("grp", "path")),
            P(("grp", "path"), None),
            P(("scen", "sub"), ("grp", "path")),
            P(("scen", "sub"), ("grp", "path")),
            P(("grp", "path")),
            P(("grp", "scen", "sub")),
        ),
        out_specs=(
            P(("scen", "sub"), ("grp", "path")),
            P(("scen", "sub"), ("grp", "path")),
            P(("grp", "path")),
        ),
        check_vma=False,
    )
```

```python
import jax
import jax.numpy as jnp
from jax import lax
from jax.experimental import pallas as pl
from jax.experimental.pallas import tpu as pltpu
from jax.sharding import PartitionSpec as P

PATHS_PER_BLOCK = 128
LB = 128
MAXT = 16
COMMODITY_BLOCK = 32
S = 256

SOFTMIN_RATE = 0.25
STEP_RATE = 1.0
DEMAND_UNIT = 0.0625
MIB = 1024 * 1024

F32 = jnp.float32
BF16 = jnp.bfloat16
PACK = 16
BATCH = 16
GROUP = LB // COMMODITY_BLOCK

SCALARS = pl.BlockSpec(memory_space=pltpu.SMEM)
ARRAY = pl.BlockSpec(memory_space=pltpu.VMEM)
LISTS = 3
TOGETHER = 8
UNROLL = 28
LB_BITS = 7
COUNTED = 16


def split(x):
    high = x.astype(BF16)
    return high, (x - high.astype(F32)).astype(BF16)


def stacked(x):
    return jnp.concatenate(split(x), axis=0)


def aligned(start, size, unit):
    return pl.ds(pl.multiple_of(start * unit, unit), size)


def stay(*arrays):
    return tuple(pltpu.with_memory_space_constraint(a, pltpu.HBM) for a in arrays)


REMAIN = pl.BlockSpec(memory_space=pltpu.HBM)


def fetch(given, local, arrived):
    copies = [pltpu.make_async_copy(a, b, arrived.at[i]) for i, (a, b) in enumerate(zip(given, local))]
    for copy in copies:
        copy.start()
    return copies


def listing_kernel(tile_total, *refs):
    given, (list_ref, total_ref, same_ref, wanted_ref, kept_ref) = refs[:5], refs[5:10]
    local, arrived = refs[10:15], refs[15]
    tiles_ref, count_ref, comm_ref, demand_ref, capacity_ref = local
    copies = fetch(given, local, arrived)
    blocks = tiles_ref.shape[0]
    spare = blocks * MAXT
    for copy in copies:
        copy.wait()

    def one_block(block, entry):
        live = count_ref[block]

        def one_pair(pair, entry):
            list_ref[0, entry] = block * MAXT + 2 * pair
            list_ref[1, entry] = tiles_ref[block, 2 * pair]
            list_ref[2, entry] = jnp.where(2 * pair + 1 < live, tiles_ref[block, 2 * pair + 1], tile_total)
            return entry + 1

        return lax.fori_loop(0, (live + 1) // 2, one_pair, entry)

    entries = lax.fori_loop(0, blocks, one_block, 0)
    batches = (entries + BATCH - 1) // BATCH
    total_ref[0] = batches
    total_ref[1] = (entries + COUNTED - 1) // COUNTED

    def pad(entry, carry):
        list_ref[0, entry] = spare
        list_ref[1, entry] = tile_total
        list_ref[2, entry] = tile_total
        return carry

    lax.fori_loop(entries, batches * BATCH, pad, 0)
    kept_ref[...] = capacity_ref[...]

    commodity_rows = lax.broadcasted_iota(jnp.int32, (LB, PATHS_PER_BLOCK), 0)
    for block in range(blocks):
        group, j = block // GROUP, block % GROUP
        demand = demand_ref[:, group * LB : (group + 1) * LB].astype(F32).astype(BF16)
        onehot = (commodity_rows == comm_ref[block : block + 1, :] + COMMODITY_BLOCK * j).astype(F32).astype(BF16)
        same = lax.dot_general(onehot, onehot, (((0,), (0,)), ((), ())), preferred_element_type=F32)
        same_ref[block] = same.astype(BF16)
        wanted_ref[block] = jnp.dot(demand, onehot, preferred_element_type=F32) * DEMAND_UNIT


def build_listing(tile_total, block_tiles, block_count, path_commodity, demand, capacity):
    blocks = block_tiles.shape[0]
    given = stay(block_tiles, block_count, path_commodity, demand, capacity.reshape(-1, LB))
    return pl.pallas_call(
        lambda *refs: listing_kernel(tile_total, *refs),
        in_specs=[REMAIN] * 5,
        out_specs=[SCALARS, SCALARS, ARRAY, ARRAY, ARRAY],
        out_shape=[
            jax.ShapeDtypeStruct((LISTS, blocks * MAXT // 2 + BATCH), jnp.int32),
            jax.ShapeDtypeStruct((2,), jnp.int32),
            jax.ShapeDtypeStruct((blocks, PATHS_PER_BLOCK, PATHS_PER_BLOCK), BF16),
            jax.ShapeDtypeStruct((blocks, demand.shape[0], PATHS_PER_BLOCK), F32),
            jax.ShapeDtypeStruct(given[4].shape, F32),
        ],
        scratch_shapes=[pltpu.SMEM(a.shape, a.dtype) for a in given[:2]]
        + [pltpu.VMEM(a.shape, a.dtype) for a in given[2:]]
        + [pltpu.SemaphoreType.DMA((5,))],
        compiler_params=pltpu.CompilerParams(vmem_limit_bytes=8 * MIB),
        cost_estimate=pl.CostEstimate(flops=10**9, bytes_accessed=10**7, transcendentals=0),
        name="listing",
    )(*given)


def incidence_kernel(list_ref, total_ref, given_ref, hits_ref, turned_ref, links_ref, arrived):
    copies = fetch([given_ref], [links_ref], arrived)
    blocks = links_ref.shape[1] // PATHS_PER_BLOCK
    for ref in (hits_ref, turned_ref):
        ref[-2 * LB :, :] = jnp.zeros((2 * LB, LB), BF16)
    lanes = [(lax.broadcasted_iota(jnp.int32, (PACK, LB), 0) + PACK * g).astype(F32).astype(BF16) for g in range(LB // PACK)]
    one, zero = jnp.ones((PACK, PATHS_PER_BLOCK), BF16), jnp.zeros((PACK, PATHS_PER_BLOCK), BF16)
    copies[0].wait()

    def count_step(step, carry):
        done = []
        for j in range(COUNTED):
            entry = step * COUNTED + j
            slot = list_ref[0, entry]
            block = jnp.minimum(slot // MAXT, blocks - 1)
            links = links_ref[:, aligned(block, PATHS_PER_BLOCK, PATHS_PER_BLOCK)]
            for side in range(2):
                place = (links - list_ref[1 + side, entry] * LB).astype(F32)
                counts = None
                for h in range(links.shape[0]):
                    row = jnp.broadcast_to(place[h : h + 1, :], (PACK, PATHS_PER_BLOCK)).astype(BF16)
                    hit = [jnp.where(row == lane, one, zero) for lane in lanes]
                    counts = hit if counts is None else [a + b for a, b in zip(counts, hit)]
                done.append((aligned(slot + side, LB, LB), jnp.concatenate(counts, axis=0)))
        for where, table in done:
            hits_ref[where, :] = table
            turned_ref[where, :] = table.T
        return carry

    lax.fori_loop(0, total_ref[1], count_step, 0)


def build_incidence(path_links, pairs, total):
    blocks = path_links.shape[1] // PATHS_PER_BLOCK
    slots = blocks * MAXT + 2
    return pl.pallas_call(
        incidence_kernel,
        in_specs=[SCALARS, SCALARS, REMAIN],
        out_specs=[ARRAY, ARRAY],
        out_shape=[
            jax.ShapeDtypeStruct((slots * LB, PATHS_PER_BLOCK), BF16),
            jax.ShapeDtypeStruct((slots * PATHS_PER_BLOCK, LB), BF16),
        ],
        scratch_shapes=[pltpu.VMEM(path_links.shape, path_links.dtype), pltpu.SemaphoreType.DMA((1,))],
        compiler_params=pltpu.CompilerParams(vmem_limit_bytes=8 * MIB),
        cost_estimate=pl.CostEstimate(flops=10**6, bytes_accessed=20 * 10**6, transcendentals=0),
        name="incidence",
    )(pairs, total, *stay(path_links))


def sweep(list_ref, total_ref, hits_ref, turned_ref, same_ref, wanted_at, put_flow, split_ref, cost_ref, flow_ref, load_ref):
    blocks, rows2 = same_ref.shape[0], cost_ref.shape[1]
    rows = rows2 // 2
    flow_ref[blocks] = jnp.zeros(flow_ref.shape[1:], BF16)
    split_ref[split_ref.shape[0] - 1] = jnp.zeros(split_ref.shape[1:], BF16)
    load_ref[...] = jnp.zeros_like(load_ref)
    cost_ref[...] = jnp.zeros_like(cost_ref)
    batches = total_ref[0]

    def cost_batch(batch, carry):
        done = []
        for j in range(BATCH):
            slot, left, right = (list_ref[i, batch * BATCH + j] for i in range(LISTS))
            block = slot // MAXT
            chosen = jnp.concatenate([split_ref[left], split_ref[right]], axis=1)
            done.append((block, jnp.dot(chosen, hits_ref[aligned(slot, 2 * LB, LB), :], preferred_element_type=F32)))
        for block, cost in done:
            cost_ref[block] += cost
        return carry

    lax.fori_loop(0, batches, cost_batch, 0)

    for block in range(blocks):
        weight = jnp.exp(-SOFTMIN_RATE * (cost_ref[block, :rows] + cost_ref[block, rows:]))
        total = jnp.dot(stacked(weight), same_ref[block], preferred_element_type=F32)
        flow = wanted_at(block) * weight / (total[:rows] + total[rows:])
        put_flow(block, flow)
        flow_ref[block] = stacked(flow)

    def load_batch(batch, carry):
        done = []
        for j in range(BATCH):
            slot, left, right = (list_ref[i, batch * BATCH + j] for i in range(LISTS))
            block = slot // MAXT
            for side, tile in enumerate((left, right)):
                turned = turned_ref[aligned(slot + side, LB, LB), :]
                done.append((tile, jnp.dot(flow_ref[block], turned, preferred_element_type=F32)))
        for tile, load in done:
            load_ref[tile] += load
        return carry

    lax.fori_loop(0, batches, load_batch, 0)


def spread(split_ref, first, shard):
    for k in range(shard.shape[-1] // LB):
        split_ref[first + k] = stacked(shard[:, k * LB : (k + 1) * LB])


def path_columns(block):
    return slice(block * PATHS_PER_BLOCK, (block + 1) * PATHS_PER_BLOCK)


def sweep_scratch(rows, tiles, blocks):
    return [
        pltpu.VMEM((tiles + 1, 2 * rows, LB), BF16),
        pltpu.VMEM((blocks + 1, 2 * rows, PATHS_PER_BLOCK), F32),
        pltpu.VMEM((blocks + 1, 2 * rows, PATHS_PER_BLOCK), BF16),
        pltpu.VMEM((tiles + 1, 2 * rows, LB), F32),
    ]


def sweep_cost(size):
    return pl.CostEstimate(flops=10**10, bytes_accessed=size, transcendentals=0)


def half_kernel(far, n, list_ref, total_ref, *refs):
    pieces, (hits_ref, turned_ref, same_ref, wanted_ref, capacity_ref) = refs[:n], refs[n : n + 5]
    flows_ref, mine_ref, other_ref, *scratch = refs[-7:]
    z = lax.axis_index("path")
    rows = scratch[0].shape[1] // 2
    side = lax.div(z, 2)
    side = 1 - side if far else side
    shard_tiles = pieces[0].shape[1] // LB
    for m, piece in enumerate(pieces):
        start = side if piece.shape[0] == 2 * rows else 0
        spread(scratch[0], (z ^ m) * shard_tiles, piece[aligned(start, rows, rows), :])

    def wanted_at(block):
        return wanted_ref[block, aligned(side, rows, rows), :]

    def put_flow(block, flow):
        flows_ref[:, path_columns(block)] = flow

    sweep(list_ref, total_ref, hits_ref, turned_ref, same_ref, wanted_at, put_flow, *scratch)
    load_ref = scratch[3]
    height = rows // 2
    for out_ref, place in ((mine_ref, lax.rem(z, 2)), (other_ref, 1 - lax.rem(z, 2))):
        for k in range(load_ref.shape[0] - 1):
            high = load_ref[k, aligned(place, height, height), :]
            out_ref[k] = high + load_ref[k, pl.ds(pl.multiple_of(rows + place * height, height), height), :]
    for out_ref, start in ((mine_ref, 0), (other_ref, height // 2 if far else 0)):
        out_ref[load_ref.shape[0] - 1] = jnp.zeros((height, LB), F32)
        out_ref[load_ref.shape[0] - 1, start : start + shard_tiles, :] = capacity_ref[...]


def half_sweep(pieces, rows, built, capacity, far):
    hits, turned, pairs, total, same, wanted = built
    own = pieces[0].shape[1]
    n = len(pieces)
    blocks = wanted.shape[0]
    tiles = n * own // LB
    return pl.pallas_call(
        lambda *refs: half_kernel(far, n, *refs),
        in_specs=[SCALARS, SCALARS] + [ARRAY] * (n + 5),
        out_specs=[ARRAY] * 3,
        out_shape=[jax.ShapeDtypeStruct((rows, blocks * PATHS_PER_BLOCK), F32)]
        + [jax.ShapeDtypeStruct((tiles + 1, rows // 2, LB), F32)] * 2,
        scratch_shapes=sweep_scratch(rows, tiles, blocks),
        compiler_params=pltpu.CompilerParams(vmem_limit_bytes=16 * MIB),
        cost_estimate=sweep_cost(25 * 10**6),
        name="far_sweep" if far else "near_sweep",
    )(pairs, total, *pieces, hits, turned, same, wanted, capacity)


def wide_kernel(list_ref, total_ref, lengths_ref, hits_ref, turned_ref, same_ref, wanted_ref, flows_ref, out_ref, *scratch):
    shards, _, own = lengths_ref.shape
    rows = lengths_ref.shape[1]

    def one_shard(i, carry):
        spread(scratch[0], i * (own // LB), lengths_ref[i])
        return carry

    lax.fori_loop(0, shards, one_shard, 0)

    def put_flow(block, flow):
        flows_ref[:, path_columns(block)] = flow

    sweep(
        list_ref, total_ref, hits_ref, turned_ref, same_ref, lambda block: wanted_ref[block], put_flow, *scratch
    )
    out_ref[...] = scratch[3][:-1, :rows, :] + scratch[3][:-1, rows:, :]


def wide_sweep(lengths, built):
    hits, turned, pairs, total, same, wanted = built
    shards, rows, own = lengths.shape
    blocks = wanted.shape[0]
    tiles = shards * own // LB
    return pl.pallas_call(
        wide_kernel,
        in_specs=[SCALARS, SCALARS] + [ARRAY] * 5,
        out_specs=[ARRAY] * 2,
        out_shape=[
            jax.ShapeDtypeStruct((rows, blocks * PATHS_PER_BLOCK), F32),
            jax.ShapeDtypeStruct((tiles, rows, LB), F32),
        ],
        scratch_shapes=sweep_scratch(rows, tiles, blocks),
        compiler_params=pltpu.CompilerParams(vmem_limit_bytes=48 * MIB),
        cost_estimate=sweep_cost(10**7),
        name="wide_sweep",
    )(pairs, total, lengths, hits, turned, same, wanted)


def growth_kernel(n, parts, *refs):
    lengths, (capacity_ref, weight_ref) = refs[:n], refs[n : n + 2]
    loads = refs[n + 2 : n + 2 + parts]
    next_refs, mixed_ref, grown_ref = refs[-n - 2 : -2], refs[-2], refs[-1]
    z = lax.axis_index("path")
    links_total, height, _ = grown_ref.shape
    shard_tiles = links_total // n
    total = jnp.zeros((height, LB), F32)
    own, near, far = capacity_ref[...], loads[1][links_total], loads[2][links_total]
    capacities = (own, near, far, far[height // 2 :])
    for m in range(n):
        row = aligned(z if lengths[m].shape[0] == n * height else lax.rem(z, 2), height, height)
        first = (z ^ m) * shard_tiles
        for k in range(shard_tiles):
            columns = slice(k * LB, (k + 1) * LB)
            load = loads[0][first + k]
            for ref in loads[1:]:
                load = load + ref[first + k]
            grown = lengths[m][row, columns] * jnp.exp(STEP_RATE * load / capacities[m][k : k + 1])
            grown_ref[m * shard_tiles + k] = grown
            total = total + grown
    factor = (links_total * LB) / jnp.sum(total, axis=1, keepdims=True)
    weight = weight_ref[aligned(z, height, height), :]
    for m in range(n):
        first = (z ^ m) * shard_tiles
        for k in range(shard_tiles):
            new = grown_ref[m * shard_tiles + k] * factor
            next_refs[m][:, k * LB : (k + 1) * LB] = new
            mixed_ref[pl.ds(first + k, 1), :] = jnp.sum(weight * new, axis=0, keepdims=True)


def grow(loads, lengths, capacity, weights):
    n, parts = len(lengths), len(loads)
    tiles, height = loads[0].shape[0] - 1, loads[0].shape[1]
    return pl.pallas_call(
        lambda *refs: growth_kernel(n, parts, *refs),
        in_specs=[ARRAY] * (n + 2 + parts),
        out_specs=[ARRAY] * (n + 1),
        out_shape=[jax.ShapeDtypeStruct((height, tiles * LB // n), F32)] * n + [jax.ShapeDtypeStruct((tiles, LB), F32)],
        scratch_shapes=[pltpu.VMEM((tiles, height, LB), F32)],
        compiler_params=pltpu.CompilerParams(vmem_limit_bytes=8 * MIB),
        cost_estimate=pl.CostEstimate(flops=10**6, bytes_accessed=5 * 10**6, transcendentals=10**5),
        name="growth",
    )(*lengths, capacity, weights, *loads)


def robust_kernel(parts, links_ref, *refs):
    part_refs, (out_ref, mixed_ref) = refs[:parts], refs[parts:]
    blocks = out_ref.shape[0]
    hops = links_ref.shape[0]
    mixed = part_refs[0][...]
    for ref in part_refs[1:]:
        mixed = mixed + ref[...]
    mixed_ref[...] = mixed
    for first in range(0, blocks, TOGETHER):
        group = range(first, min(first + TOGETHER, blocks))
        links = [links_ref[:, path_columns(block)] for block in group]

        def one_tile(tile, costs):
            table = jnp.broadcast_to(mixed_ref[pl.ds(tile, 1), :], (hops, LB))
            found = [jnp.take_along_axis(table, x & (LB - 1), axis=1) for x in links]
            return [jnp.where((x >> LB_BITS) == tile, f, c) for x, f, c in zip(links, found, costs)]

        tiles = mixed_ref.shape[0]
        costs = [jnp.zeros((hops, PATHS_PER_BLOCK), F32)] * len(links)
        step = UNROLL if tiles % UNROLL == 0 else 1

        def some_tiles(i, costs):
            for j in range(step):
                costs = one_tile(i * step + j, costs)
            return costs

        costs = lax.fori_loop(0, tiles // step, some_tiles, costs)
        for block, cost in zip(group, costs):
            out_ref[block : block + 1, :] = jnp.sum(cost, axis=0, keepdims=True) / S


def robust_costs(path_links, parts):
    hops, paths = path_links.shape
    blocks = paths // PATHS_PER_BLOCK
    out = pl.pallas_call(
        lambda *refs: robust_kernel(len(parts), *refs),
        in_specs=[ARRAY] * (len(parts) + 1),
        out_specs=ARRAY,
        out_shape=jax.ShapeDtypeStruct((blocks, PATHS_PER_BLOCK), F32),
        scratch_shapes=[pltpu.VMEM(parts[0].shape, F32)],
        compiler_params=pltpu.CompilerParams(vmem_limit_bytes=8 * MIB),
        cost_estimate=pl.CostEstimate(flops=10**6, bytes_accessed=10**6, transcendentals=0),
        name="robust",
    )(path_links, *parts)
    return out.reshape(-1)


def exchange(x, axis, n, bit):
    return lax.ppermute(x, axis, [(i, i ^ bit) for i in range(n)])


def body_paired(sizes, path_links, block_tiles, block_count, path_commodity, demand, lengths, capacity, scenario_weight):
    n = sizes["path"]
    rows, own = lengths.shape
    half, height = rows // 2, rows // n
    z = lax.axis_index("path").astype(jnp.int32)
    side = z // 2
    far = lax.dynamic_slice(lengths, ((1 - side) * half, 0), (half, own))
    near = lax.dynamic_slice(lengths, (side * half, 0), (half, own))

    def swap(x, m):
        return exchange(x, "path", n, m)

    lengths, far, near = lax.optimization_barrier((lengths, far, near))
    near_straight, near_crossed = swap(near, 2), swap(near, 3)
    pairs, total, same, wanted, capacity_tiles = build_listing(
        n * own // LB, block_tiles, block_count, path_commodity, demand, capacity
    )
    late, same = lax.optimization_barrier((far, same))
    shared = swap(lengths, 1)
    far_pieces = [far, shared, near_straight, near_crossed]
    near_pieces = [near, shared, swap(late, 2), swap(late, 3)]
    built = (*build_incidence(path_links, pairs, total), pairs, total, same, wanted)
    far_flows, straight, crossed = half_sweep(far_pieces, half, built, capacity_tiles, True)
    partial = straight + swap(crossed, 1)
    near_flows, mine, other = half_sweep(near_pieces, half, built, capacity_tiles, False)
    partial, other, near_flows = lax.optimization_barrier((partial, other, near_flows))
    loads = [mine, swap(other, 1), swap(partial, 2)]
    first, second = jnp.where(side == 0, near_flows, far_flows), jnp.where(side == 0, far_flows, near_flows)
    flows = jnp.concatenate([first, second], axis=0)
    weight_column = scenario_weight[:, None]
    flows, weight_column = lax.optimization_barrier((flows, weight_column))
    *new, mixed = grow(loads, near_pieces, capacity_tiles, weight_column)
    mixed = mixed + exchange(mixed, "sub", 2, 1)
    mixed, *new[1:] = lax.optimization_barrier((mixed, *new[1:]))
    diagonal = exchange(mixed, ("path", "scen"), 2 * n, 3)
    mixed = mixed + exchange(mixed, "scen", 2, 1) + swap(mixed, 1) + diagonal
    parts = [mixed, swap(mixed, 2)]
    arrived = [new[0]] + [swap(new[m], m) for m in range(1, n)]
    lengths_next = jnp.zeros((rows, own), F32)
    for m in range(n):
        lengths_next = lax.dynamic_update_slice(lengths_next, arrived[m], ((z ^ m) * height, 0))
    parts[1], lengths_next = lax.optimization_barrier((parts[1], lengths_next))
    robust = robust_costs(path_links, parts)
    return flows, lengths_next, robust


def body_wide(sizes, path_links, block_tiles, block_count, path_commodity, demand, lengths, capacity, scenario_weight):
    gathered = lax.all_gather(lengths, "path", axis=0, tiled=False)
    tiles = gathered.shape[0] * gathered.shape[2] // LB
    pairs, total, same, wanted, _ = build_listing(tiles, block_tiles, block_count, path_commodity, demand, capacity)
    built = (*build_incidence(path_links, pairs, total), pairs, total, same, wanted)
    flows, loads = wide_sweep(gathered, built)
    loads = loads.transpose(1, 0, 2).reshape(lengths.shape[0], -1)
    own_loads = lax.psum_scatter(loads, "path", scatter_dimension=1, tiled=True)
    grown = lengths * jnp.exp(STEP_RATE * own_loads / capacity[None, :])
    totals = lax.psum(jnp.sum(grown, axis=1), "path")
    lengths_next = grown * (loads.shape[1] / totals)[:, None]
    mixed = lax.psum(jnp.sum(lengths_next * scenario_weight[:, None], axis=0), ("scen", "sub"))
    mixed = lax.all_gather(mixed.reshape(-1, LB), "path", axis=0, tiled=True)
    return flows, lengths_next, robust_costs(path_links, [mixed])


def solution(mesh):
    sizes = dict(mesh.shape)

    def body(*args):
        paired = sizes["path"] == 4 and sizes["scen"] == 2 and sizes["sub"] == 2 and args[5].shape[0] % 64 == 0 and args[5].shape[1] // LB <= args[5].shape[0] // 8
        return (body_paired if paired else body_wide)(sizes, *args)

    return jax.shard_map(
        body,
        mesh=mesh,
        in_specs=(
            P(None, ("grp", "path")),
            P(("grp", "path"), None),
            P(("grp", "path")),
            P(("grp", "path"), None),
            P(("scen", "sub"), ("grp", "path")),
            P(("scen", "sub"), ("grp", "path")),
            P(("grp", "path")),
            P(("grp", "scen", "sub")),
        ),
        out_specs=(
            P(("scen", "sub"), ("grp", "path")),
            P(("scen", "sub"), ("grp", "path")),
            P(("grp", "path")),
        ),
        check_vma=False,
    )
```
